128 devices in a mesh: member: 16 (over z_lo, y, core), tile: 8 (over z_hi, x).
Axes of the slice: x: 4, y: 4, z: 4 (z_hi: 2, z_lo: 2; z = z_hi * 2 + z_lo), core: 2. Of those that a mesh axis runs over, the one named last changes fastest.
Arguments:
- node_fine: int32 [16, 12], P('member'), may hold values from 0 to 8
- node_coarse: int32 [64, 12], P('member'), may hold values from 0 to 8
- weight_fine: int32 [16], P('member'), may hold values from -3 to 3
- weight_coarse: int32 [64], P('member'), may hold values from -3 to 3
- mode_x: float32 [12, 128], replicated, may hold values from -1 to 1
- mode_y: float32 [12, 512], replicated, may hold values from -1 to 1
- mode_z: float32 [12, 32], replicated, may hold values from -1 to 1
- source_fine: float32 [128, 32, 512], P('tile'), may hold values from -12 to 12
- source_coarse: float32 [64, 16, 256], P(None, None, 'tile'), may hold values from -6 to 6
Outputs:
- combined: float32 [64, 16, 256], P('member', None, 'tile')
The draws below stay inside these ranges and needn't reach their ends.
All inputs are finite; a program needn't handle non-finite values.
Results may differ from the reference program's by a relative error of at most 0.00026.
Values sent between devices are 32-bit elements; how exact they have to be, the bound alone decides.
A program may use at most 192 MiB of HBM per device.

```python
import math
import jax
import jax.numpy as jnp
from jax import lax

KL = 12
NODES = 9
SWEEPS = 3
NZF = 32
NYF = 512
FINE = 16
COARSE = 64
NXF = 128
NXC = 64
NZC = 16
NYC = 256


def with_ends(array, stream_key, low, top_value):
    shape = array.shape
    place = [jax.random.randint(jax.random.fold_in(stream_key, axis), (), 0, shape[axis]) for axis in range(len(shape))]
    array = array.at[tuple(place)].set(low)
    longest = shape.index(max(shape))
    place[longest] = (place[longest] + 1) % shape[longest]
    return array.at[tuple(place)].set(top_value)


def levels(stream_key, dims, cuts, smallest, largest):
    loudness = 1.0
    for position, parts in cuts:
        heights = jax.random.uniform(jax.random.fold_in(jax.random.fold_in(stream_key, 6), position), (parts,), jnp.float32, smallest / len(cuts), largest / len(cuts))
        loudness = loudness * jnp.repeat(jnp.exp(heights), dims[position] // parts).reshape((-1,) + (1,) * (len(dims) - 1 - position))
    return loudness


def scatter_about(own_key, shape, scale, limit, shards=(), dtype=jnp.bfloat16):
    values = jax.random.normal(own_key, shape, jnp.float32) * scale
    if len(shards) > 0:
        values = levels(own_key, shape, shards, -0.22, 0.18) * values
    return jnp.clip(values, min=-limit, max=limit).astype(dtype)


def setup_inputs(seed: int = 0) -> dict:
    key_of = jax.random.split(jax.random.key(seed), 10)
    node_fine = with_ends(jax.random.randint(key_of[0], (FINE, KL), 0, NODES), jax.random.fold_in(key_of[0], 1), 0, NODES - 1).astype(jnp.int32)
    node_coarse = with_ends(jax.random.randint(key_of[1], (COARSE, KL), 0, NODES), jax.random.fold_in(key_of[1], 1), 0, NODES - 1).astype(jnp.int32)
    weight_fine = with_ends(jax.random.randint(key_of[2], (FINE,), -3, 4), jax.random.fold_in(key_of[2], 1), -3, 3).astype(jnp.int32)
    weight_coarse = with_ends(jax.random.randint(key_of[3], (COARSE,), -3, 4), jax.random.fold_in(key_of[3], 1), -3, 3).astype(jnp.int32)
    mode_x = jnp.clip(jax.random.uniform(key_of[4], (KL, NXF), jnp.float32, -1.0, 1.0), -1.0, 1.0)
    mode_y = jnp.clip(jax.random.uniform(key_of[5], (KL, NYF), jnp.float32, -1.0, 1.0), -1.0, 1.0)
    mode_z = jnp.clip(jax.random.uniform(key_of[6], (KL, NZF), jnp.float32, -1.0, 1.0), -1.0, 1.0)
    source_fine = scatter_about(key_of[7], (NXF, NZF, NYF), 2.0, 12.0, ((0, 8),), jnp.float32)
    source_coarse = scatter_about(key_of[8], (NXC, NZC, NYC), 1.0, 6.0, ((2, 8),), jnp.float32)
    return dict(node_fine=node_fine, node_coarse=node_coarse, weight_fine=weight_fine, weight_coarse=weight_coarse, mode_x=mode_x, mode_y=mode_y, mode_z=mode_z, source_fine=source_fine, source_coarse=source_coarse)


CENTRE = 1.125
HALF_WIDTH = 0.875
SPREAD_RATIO = CENTRE / HALF_WIDTH


def sweep_factors(sweep_count):
    previous = 1.0 / SPREAD_RATIO
    factors = []
    for _ in range(sweep_count - 1):
        current = 1.0 / (2.0 * SPREAD_RATIO - previous)
        factors.append((current * previous, 2.0 * current / HALF_WIDTH))
        previous = current
    return factors


def shifted(tensor, spatial, along_dim, offset):
    for current in spatial:
        begin_at = offset if current == along_dim else 1
        tensor = lax.slice_in_dim(tensor, begin_at, tensor.shape[current] - 2 + begin_at, axis=current)
    return tensor


def diagonal_of(cond_pad, spatial):
    centre = shifted(cond_pad, spatial, -1, 1)
    running = jnp.zeros_like(centre)
    for along_dim in spatial:
        for offset in (0, 2):
            running = running + 0.5 * (centre + shifted(cond_pad, spatial, along_dim, offset))
    return running


def apply_op(field_pad, cond_pad, spatial):
    centre_k = shifted(cond_pad, spatial, -1, 1)
    centre_v = shifted(field_pad, spatial, -1, 1)
    running = jnp.zeros_like(centre_v * centre_k)
    for along_dim in spatial:
        for offset in (0, 2):
            coupling = 0.5 * (centre_k + shifted(cond_pad, spatial, along_dim, offset))
            running = running + coupling * (centre_v - shifted(field_pad, spatial, along_dim, offset))
    return running


def node_values(node_index):
    return jnp.cos(math.pi * node_index.astype(jnp.float32) / (NODES - 1))


def pair_mean(modes):
    return 0.5 * (modes[:, 0::2] + modes[:, 1::2])


def log_field(values, along_x, along_z, along_y):
    weighted = (along_x.T * values)[:, None, :] * along_z.T[None, :, :]
    flattened = weighted.reshape(weighted.shape[0] * weighted.shape[1], weighted.shape[2])
    product = jnp.dot(flattened, along_y, precision=lax.Precision.HIGHEST)
    return product.reshape(weighted.shape[0], weighted.shape[1], along_y.shape[1])


def restrict(tensor):
    blocks = tensor.reshape(tensor.shape[0] // 2, 2, tensor.shape[1] // 2, 2, tensor.shape[2] // 2, 2)
    return blocks.sum(axis=(1, 3, 5)) * 0.125


def solve_member(source, conduct):
    spatial = (0, 1, 2)
    cond_pad = jnp.pad(conduct, 1)
    diagonal = diagonal_of(cond_pad, spatial)
    update = source / (CENTRE * diagonal)
    result = update
    residual = source
    for keep_part, push_part in sweep_factors(SWEEPS):
        residual = residual - apply_op(jnp.pad(update, 1), cond_pad, spatial)
        update = keep_part * update + push_part * residual / diagonal
        result = result + update
    return result


def reference(node_fine, node_coarse, weight_fine, weight_coarse, mode_x, mode_y, mode_z, source_fine, source_coarse):
    mode_xc = pair_mean(mode_x)
    mode_yc = pair_mean(mode_y)
    mode_zc = pair_mean(mode_z)

    def fine_step(running, member_item):
        node_index, weight = member_item
        conduct = jnp.exp(log_field(node_values(node_index), mode_x, mode_z, mode_y))
        solved = solve_member(source_fine, conduct)
        return running + weight.astype(jnp.float32) * restrict(solved), None

    def coarse_step(running, member_item):
        node_index, weight = member_item
        conduct = jnp.exp(log_field(node_values(node_index), mode_xc, mode_zc, mode_yc))
        solved = solve_member(source_coarse, conduct)
        return running + weight.astype(jnp.float32) * solved, None

    running = jnp.zeros((NXC, NZC, NYC), jnp.float32)
    running, ignored = lax.scan(fine_step, running, (node_fine, weight_fine))
    running, ignored = lax.scan(coarse_step, running, (node_coarse, weight_coarse))
    return running
```

```python
import math

import jax
import jax.numpy as jnp
from jax import lax
from jax.experimental import pallas as pl
from jax.experimental.pallas import tpu as pltpu
from jax.sharding import PartitionSpec as P

NODES = 9
SWEEPS = 3
CENTRE = 1.125
HALF_WIDTH = 0.875
SPREAD_RATIO = CENTRE / HALF_WIDTH
LOG2E = 1.0 / math.log(2.0)

F32 = jnp.float32
BF16 = jnp.bfloat16
MESH = pl.DeviceIdType.MESH

TILES = 8
MEMBERS = 16
KL = 12
KP = 16
XS = 16
XC = 8
XPAD = 8


def sweep_factors(sweep_count):
    previous = 1.0 / SPREAD_RATIO
    factors = []
    for _ in range(sweep_count - 1):
        current = 1.0 / (2.0 * SPREAD_RATIO - previous)
        factors.append((current * previous, 2.0 * current / HALF_WIDTH))
        previous = current
    return factors


(KEEP1, PUSH1), (KEEP2, PUSH2) = sweep_factors(SWEEPS)
FIRST = 1.0 / CENTRE


def iota(shape, dim):
    return lax.broadcasted_iota(jnp.int32, shape, dim)


def halves(value):
    high = value.astype(BF16)
    return high, (value - high.astype(F32)).astype(BF16)


def thirds(value):
    high = value.astype(BF16)
    rest = value - high.astype(F32)
    middle = rest.astype(BF16)
    return high, middle, (rest - middle.astype(F32)).astype(BF16)


def stencil(below, here, above, masks):
    lane_first, lane_last, sub_first, sub_last = masks
    dims = here.ndim
    ka, ja, sa, la = dims - 4, dims - 3, dims - 2, dims - 1
    nk, nj = here.shape[ka], here.shape[ja]

    def part(low, high, axis):
        return lax.slice_in_dim(here, low, high, axis=axis)

    k_wrap = jnp.where(lane_first, 0.0, pltpu.roll(part(nk - 1, nk, ka), 1, la))
    k_down = jnp.concatenate([k_wrap, part(0, nk - 1, ka)], ka)
    k_wrap = jnp.where(lane_last, 0.0, pltpu.roll(part(0, 1, ka), 127, la))
    k_up = jnp.concatenate([part(1, nk, ka), k_wrap], ka)
    j_wrap = jnp.where(sub_first, 0.0, pltpu.roll(part(nj - 1, nj, ja), 1, sa))
    j_down = jnp.concatenate([j_wrap, part(0, nj - 1, ja)], ja)
    j_wrap = jnp.where(sub_last, 0.0, pltpu.roll(part(0, 1, ja), 7, sa))
    j_up = jnp.concatenate([part(1, nj, ja), j_wrap], ja)
    return ((below + above) + (k_down + k_up)) + (j_down + j_up)


def node_column(node_row):
    index = node_row
    value = jnp.zeros(node_row.shape, F32)
    for node in range(NODES):
        value = jnp.where(index == node, math.cos(math.pi * node / (NODES - 1)) * LOG2E, value)
    spread = jnp.broadcast_to(value, (KP, KL))
    own = iota((KP, KL), 0) == iota((KP, KL), 1)
    return jnp.sum(jnp.where(own, spread, 0.0), axis=1, keepdims=True)


def block_transpose(blocks, width, lanes):
    count = len(blocks)
    place = lanes // width
    blocks = list(blocks)
    bit = 1
    while bit < count:
        clear = (place & bit) == 0
        for low in range(count):
            if low & bit:
                continue
            a, b = blocks[low], blocks[low | bit]
            blocks[low] = jnp.where(clear, a, pltpu.roll(b, width * bit, 1))
            blocks[low | bit] = jnp.where(clear, pltpu.roll(a, 128 - width * bit, 1), b)
        bit *= 2
    return blocks


def kernel(
    node_f,
    node_c,
    w_f,
    w_c,
    mode_x,
    mode_y,
    mode_z,
    src_f,
    src_c,
    out,
    fraw,
    craw,
    cpack,
    cgot,
    mpad,
    xt,
    zt,
    perm_f,
    perm_c,
    rhs_f,
    rhs_c,
    logs_f,
    logs_c,
    c_f,
    f_f,
    inv_f,
    d_f,
    w0_f,
    e_f,
    w1_f,
    a_f,
    u_f,
    c_c,
    f_c,
    inv_c,
    d_c,
    w0_c,
    e_c,
    w1_c,
    a_c,
    u_c,
    tot,
    sendbuf,
    recvbuf,
    local_sem,
    halo_send,
    halo_recv,
    cs_send,
    cs_recv,
    fin_send,
    fin_recv,
):
    me_m = lax.axis_index("member")
    me_t = lax.axis_index("tile")

    def to(member, tile):
        return {"member": member, "tile": tile}

    barrier = pltpu.get_barrier_semaphore()
    for step in range(1, TILES):
        pl.semaphore_signal(
            barrier,
            inc=1,
            device_id=to(me_m, lax.rem(me_t + step, TILES)),
            device_id_type=MESH,
        )
    feeding_tile = me_m // 2
    for source in range(MEMBERS):

        @pl.when(jnp.logical_not((source == me_m) & (feeding_tile == me_t)))
        def _():
            pl.semaphore_signal(
                barrier, inc=1, device_id=to(source, feeding_tile), device_id_type=MESH
            )

    own_c = pltpu.make_async_copy(src_c, craw, local_sem.at[4])
    own_c.start()
    own_f = []
    for q in range(4):
        copy = pltpu.make_async_copy(
            src_f.at[:, :, pl.ds(128 * q, 128)], fraw.at[pl.ds(2, XS), q], local_sem.at[q]
        )
        copy.start()
        own_f.append(copy)

    lanes = iota((8, 128), 1)
    subs = iota((8, 128), 0)
    masks = (lanes == 0, lanes == 127, subs == 0, subs == 7)

    own_c.wait()
    cpack[0] = jnp.zeros((8, 128), F32)
    cpack[33] = jnp.zeros((8, 128), F32)

    def pack(pair, carry):
        cpack[pair + 1] = jnp.concatenate(
            [craw[2 * pair + a, pl.ds(j, 8, stride=2), :] for a in range(2) for j in range(2)], 1
        )
        return carry

    lax.fori_loop(0, 32, pack, 0, unroll=4)

    pl.semaphore_wait(barrier, 23 - (feeding_tile == me_t).astype(jnp.int32))

    has_left = me_t > 0
    has_right = me_t < TILES - 1

    def halo_copy(q, rightwards):
        if rightwards:
            return pltpu.make_async_remote_copy(
                src_ref=src_f.at[pl.ds(XS - 2, 2), :, pl.ds(128 * q, 128)],
                dst_ref=fraw.at[pl.ds(0, 2), q],
                send_sem=halo_send.at[q],
                recv_sem=halo_recv.at[q],
                device_id=to(me_m, lax.rem(me_t + 1, TILES)),
                device_id_type=MESH,
            )
        return pltpu.make_async_remote_copy(
            src_ref=src_f.at[pl.ds(0, 2), :, pl.ds(128 * q, 128)],
            dst_ref=fraw.at[pl.ds(XS + 2, 2), q],
            send_sem=halo_send.at[4 + q],
            recv_sem=halo_recv.at[4 + q],
            device_id=to(me_m, lax.rem(me_t + TILES - 1, TILES)),
            device_id_type=MESH,
        )

    @pl.when(has_right)
    def _():
        for q in range(4):
            halo_copy(q, True).start()

    @pl.when(has_left)
    def _():
        for q in range(4):
            halo_copy(q, False).start()

    @pl.when(jnp.logical_not(has_left))
    def _():
        fraw[0:2] = jnp.zeros((2, 4, 32, 128), F32)

    @pl.when(jnp.logical_not(has_right))
    def _():
        fraw[XS + 2 : XS + 4] = jnp.zeros((2, 4, 32, 128), F32)

    def strip_copy(step):
        there = lax.rem(me_t + step, TILES)
        return pltpu.make_async_remote_copy(
            src_ref=cpack.at[pl.ds(4 * there, 6)],
            dst_ref=cgot.at[me_t],
            send_sem=cs_send.at[step],
            recv_sem=cs_recv.at[step],
            device_id=to(me_m, there),
            device_id_type=MESH,
        )

    for step in range(1, TILES):
        strip_copy(step).start()
    cgot[me_t] = cpack[pl.ds(4 * me_t, 6)]

    col = iota((512, 512), 1)
    match = iota((512, 512), 0) == 4 * (col & 127) + (col >> 7)
    moved = jnp.where(match, 2.0, 0.0).astype(BF16)
    perm_f[0:512] = moved
    perm_f[512:1024] = moved
    col = iota((256, 256), 1)
    match = iota((256, 256), 0) == 2 * (col & 127) + (col >> 7)
    moved = jnp.where(match, 2.0, 0.0).astype(BF16)
    perm_c[0:256] = moved
    perm_c[256:512] = moved

    mpad[...] = jnp.zeros(mpad.shape, F32)
    mpad[0:KL, :] = mode_y[...]
    my_parts = thirds(mpad[...])
    my = 0.5 * sum(
        jnp.dot(part, perm_f[0:512], preferred_element_type=F32) for part in my_parts
    )
    mpad[0:KL, 0:128] = mode_x[...]
    stacked = jnp.concatenate([mpad[:, 0:128]] * 8, 0)
    xt[...] = jnp.zeros(xt.shape, F32)
    xt[XPAD : XPAD + 128, :] = stacked.T
    mpad[0:KL, 0:32] = mode_z[...]
    stacked = jnp.concatenate([mpad[:, 0:32]] * 8, 0)
    zt[...] = stacked.T
    zf = [zt[pl.ds(j, 8, stride=4), :] for j in range(4)]
    zc = [0.5 * (zf[2 * j] + zf[2 * j + 1]) for j in range(2)]
    zf = jnp.concatenate(zf, 0)
    zc = jnp.concatenate(zc, 0)

    def sides(value):
        high, low = halves(value)
        return jnp.concatenate([high, low, high, low], 0)

    rhs_f[...] = jnp.zeros(rhs_f.shape, BF16)
    rhs_c[...] = jnp.zeros(rhs_c.shape, BF16)
    rhs_f[0:64, :] = sides(my * node_column(node_f[...]))
    myc = jnp.concatenate(
        [0.5 * (my[:, 256 * k : 256 * k + 128] + my[:, 256 * k + 128 : 256 * k + 256]) for k in range(2)], 1
    )
    for m in range(4):
        rhs_c[0:64, 256 * m : 256 * m + 256] = sides(myc * node_column(node_c[m : m + 1, :]))

    def left(value):
        high = value.astype(BF16).astype(F32)
        group = iota(value.shape, 1)
        return jnp.where(group < 32, high, value - high).astype(BF16)

    x0 = me_t * XS

    rows = []
    for i in range(XS + 6):
        rows.append(left(xt[pl.ds(x0 - 3 + XPAD + i, 1), :] * zf))
    logs_f[...] = jnp.dot(
        jnp.concatenate(rows, 0), rhs_f[...], preferred_element_type=F32
    )

    def cond_fine(i, carry):
        x = x0 - 3 + i
        inside = ((x >= 0) & (x < XS * TILES)).astype(F32)
        base = pl.multiple_of(i * 32, 32)
        for k in range(4):
            for j in range(4):
                c_f[i, k, j] = (
                    jnp.exp2(logs_f[pl.ds(base + 8 * j, 8), 128 * k : 128 * k + 128]) * inside
                )
        return carry

    lax.fori_loop(0, XS + 6, cond_fine, 0)

    rows = []
    for i in range(XC + 6):
        at = x0 - 6 + XPAD + 2 * i
        mean = 0.5 * (xt[pl.ds(at, 1), :] + xt[pl.ds(at + 1, 1), :])
        rows.append(left(mean * zc))
    logs_c[...] = jnp.dot(
        jnp.concatenate(rows, 0), rhs_c[...], preferred_element_type=F32
    )

    xc0 = me_t * XC

    def cond_coarse(i, carry):
        x = xc0 - 3 + i
        inside = ((x >= 0) & (x < XC * TILES)).astype(F32)
        base = pl.multiple_of(i * 16, 16)
        for m in range(4):
            for k in range(2):
                for j in range(2):
                    at = 256 * m + 128 * k
                    c_c[i, m, k, j] = (
                        jnp.exp2(logs_c[pl.ds(base + 8 * j, 8), at : at + 128]) * inside
                    )
        return carry

    lax.fori_loop(0, XC + 6, cond_coarse, 0)

    for copy in own_f:
        copy.wait()

    @pl.when(has_left)
    def _():
        for q in range(4):
            halo_copy(q, True).wait_recv()

    @pl.when(has_right)
    def _():
        for q in range(4):
            halo_copy(q, False).wait_recv()

    def source_fine(chunk, carry):
        rows = []
        for i in range(5):
            for j in range(4):
                rows.append(
                    jnp.concatenate(
                        [fraw[5 * chunk + i, q, pl.ds(j, 8, stride=4), :] for q in range(4)], 1
                    )
                )
        high, low = halves(jnp.concatenate(rows, 0))
        got = jnp.dot(
            jnp.concatenate([high, low], 1), perm_f[...], preferred_element_type=F32
        )
        for i in range(5):
            for k in range(4):
                for j in range(4):
                    f_f[5 * chunk + i, k, j] = got[
                        32 * i + 8 * j : 32 * i + 8 * j + 8, 128 * k : 128 * k + 128
                    ]
        return carry

    lax.fori_loop(0, 4, source_fine, 0)

    def start(i, offset, x_first, x_count, c, f, inv, d, w0, fine):
        x = x_first + i
        inside = (x >= 0) & (x < x_count)
        here = c[i + 1]
        total = 6.0 * here + stencil(c[i], here, c[i + 2], masks)
        turned = pltpu.reciprocal(total, approx=True)
        turned = turned * (2.0 - total * turned)
        turned = jnp.where(inside, turned, 0.0)
        inv[i] = turned
        source = f[i] if fine else f[i][None]
        first = (FIRST * source) * turned
        d[i] = first
        w0[i] = here * first

    def middle(i, c, f, inv, d, w0, e, w1, a, u, fine):
        source = f[i + 1] if fine else f[i + 1][None]
        here, prev = c[i + 2], d[i + 1]
        push = here * stencil(d[i], prev, d[i + 2], masks) + stencil(
            w0[i], w0[i + 1], w0[i + 2], masks
        )
        residual = (1.0 - FIRST) * source + push
        step = KEEP1 * prev + PUSH1 * (residual * inv[i + 1])
        e[i] = step
        w1[i] = here * step
        a[i] = (1.0 - PUSH1) * residual - (KEEP1 * FIRST) * source
        u[i] = prev + (1.0 + KEEP2) * step

    def finish(i, c, inv, e, w1, a, u):
        here = c[i + 3]
        push = here * stencil(e[i], e[i + 1], e[i + 2], masks) + stencil(
            w1[i], w1[i + 1], w1[i + 2], masks
        )
        residual = a[i + 1] + push
        return u[i + 1] + PUSH2 * (residual * inv[i + 2])

    def start_fine(i, carry):
        start(i, 0, x0 - 2, XS * TILES, c_f, f_f, inv_f, d_f, w0_f, True)
        return carry

    lax.fori_loop(0, XS + 4, start_fine, 0)

    def middle_fine(i, carry):
        middle(i, c_f, f_f, inv_f, d_f, w0_f, e_f, w1_f, a_f, u_f, True)
        return carry

    lax.fori_loop(0, XS + 2, middle_fine, 0)

    for step in range(1, TILES):
        strip_copy(step).wait_recv()
    rows = []
    for pair in range(6):
        sides_of = [
            block_transpose([cgot[4 * half + q, pair] for q in range(4)], 32, lanes)
            for half in range(2)
        ]
        for g in range(4):
            rows.append(jnp.concatenate([sides_of[0][g], sides_of[1][g]], 1))
    high, low = halves(jnp.concatenate(rows, 0))
    got = jnp.dot(jnp.concatenate([high, low], 1), perm_c[...], preferred_element_type=F32)
    for i in range(XC + 4):
        for k in range(2):
            for j in range(2):
                at = 16 * i + 8 * j
                f_c[i, k, j] = got[at : at + 8, 128 * k : 128 * k + 128]

    def start_coarse(i, carry):
        start(i, 0, xc0 - 2, XC * TILES, c_c, f_c, inv_c, d_c, w0_c, False)
        return carry

    lax.fori_loop(0, XC + 4, start_coarse, 0)

    def middle_coarse(i, carry):
        middle(i, c_c, f_c, inv_c, d_c, w0_c, e_c, w1_c, a_c, u_c, False)
        return carry

    lax.fori_loop(0, XC + 2, middle_coarse, 0)

    weight_f = w_f[0].astype(F32) * 0.125
    weight_c = [w_c[m].astype(F32) for m in range(4)]

    def finish_plane(xc, carry):
        pair = finish(2 * xc, c_f, inv_f, e_f, w1_f, a_f, u_f) + finish(
            2 * xc + 1, c_f, inv_f, e_f, w1_f, a_f, u_f
        )
        coarse = finish(xc, c_c, inv_c, e_c, w1_c, a_c, u_c)
        for k in range(2):
            for j in range(2):
                block = (pair[2 * k, 2 * j] + pair[2 * k + 1, 2 * j]) + (
                    pair[2 * k, 2 * j + 1] + pair[2 * k + 1, 2 * j + 1]
                )
                block = weight_f * block
                for m in range(4):
                    block = block + weight_c[m] * coarse[m, k, j]
                tot[xc, k, j] = block
        return carry

    def piece_copy(e, t):
        return pltpu.make_async_remote_copy(
            src_ref=sendbuf.at[e, t],
            dst_ref=recvbuf.at[me_m],
            send_sem=fin_send.at[e, t],
            recv_sem=fin_recv.at[me_m],
            device_id=to(2 * me_t + e, t),
            device_id_type=MESH,
        )

    def is_own(e, t):
        return (me_m == 2 * me_t + e) & (me_t == t)

    for e in range(2):
        lax.fori_loop(4 * e, 4 * e + 4, finish_plane, 0)
        for chi in range(2):
            pieces = block_transpose(
                [
                    tot[4 * e + 2 * chi + a, k, j]
                    for a in range(2)
                    for j in range(2)
                    for k in range(2)
                ],
                16,
                lanes,
            )
            for t in range(TILES):
                sendbuf[e, t, chi] = pieces[t]
        for t in range(TILES):

            @pl.when(is_own(e, t))
            def _():
                recvbuf[me_m] = sendbuf[e, t]

            @pl.when(jnp.logical_not(is_own(e, t)))
            def _():
                piece_copy(e, t).start()

    @pl.when(has_right)
    def _():
        for q in range(4):
            halo_copy(q, True).wait_send()

    @pl.when(has_left)
    def _():
        for q in range(4):
            halo_copy(q, False).wait_send()

    for step in range(1, TILES):
        strip_copy(step).wait_send()

    for source in range(MEMBERS):

        @pl.when(jnp.logical_not((source == me_m) & (feeding_tile == me_t)))
        def _():
            pltpu.make_async_remote_copy(
                src_ref=sendbuf.at[0, 0],
                dst_ref=recvbuf.at[source],
                send_sem=fin_send.at[0, 0],
                recv_sem=fin_recv.at[source],
                device_id=to(source, feeding_tile),
                device_id_type=MESH,
            ).wait_recv()

    total = recvbuf[0]
    for source in range(1, MEMBERS):
        total = total + recvbuf[source]
    row = iota((128, 128), 0)
    colm = iota((128, 128), 1)
    target = (row & 96) + 2 * (row & 15) + ((row >> 4) & 1)
    order = jnp.where(target == colm, 1.0, 0.0).astype(BF16)
    flat = total.reshape(16, 128)
    flat = sum(jnp.dot(part, order, preferred_element_type=F32) for part in thirds(flat))
    for chi in range(2):
        for g in range(4):
            out[2 * chi + g // 2, pl.ds(g % 2, 8, stride=2), :] = flat[
                8 * chi : 8 * chi + 8, 32 * g : 32 * g + 32
            ]

    for e in range(2):
        for t in range(TILES):

            @pl.when(jnp.logical_not(is_own(e, t)))
            def _():
                piece_copy(e, t).wait_send()


def body(*args):
    vmem = pl.BlockSpec(memory_space=pltpu.VMEM)
    smem = pl.BlockSpec(memory_space=pltpu.SMEM)
    hbm = pl.BlockSpec(memory_space=pl.ANY)
    fine = (4, 4, 8, 128)
    flat = (2, 2, 8, 128)
    coarse = (4, 2, 2, 8, 128)
    dma = pltpu.SemaphoreType.DMA
    scratch = [
        pltpu.VMEM((XS + 4, 4, 32, 128), F32),
        pltpu.VMEM((64, 16, 32), F32),
        pltpu.VMEM((34, 8, 128), F32),
        pltpu.VMEM((TILES, 6, 8, 128), F32),
        pltpu.VMEM((KP, 512), F32),
        pltpu.VMEM((XPAD + 128 + XPAD, 128), F32),
        pltpu.VMEM((32, 128), F32),
        pltpu.VMEM((1024, 512), BF16),
        pltpu.VMEM((512, 256), BF16),
        pltpu.VMEM((128, 512), BF16),
        pltpu.VMEM((128, 1024), BF16),
        pltpu.VMEM(((XS + 6) * 32, 512), F32),
        pltpu.VMEM(((XC + 6) * 16, 1024), F32),
        pltpu.VMEM((XS + 6,) + fine, F32),
        pltpu.VMEM((XS + 4,) + fine, F32),
        pltpu.VMEM((XS + 4,) + fine, F32),
        pltpu.VMEM((XS + 4,) + fine, F32),
        pltpu.VMEM((XS + 4,) + fine, F32),
        pltpu.VMEM((XS + 2,) + fine, F32),
        pltpu.VMEM((XS + 2,) + fine, F32),
        pltpu.VMEM((XS + 2,) + fine, F32),
        pltpu.VMEM((XS + 2,) + fine, F32),
        pltpu.VMEM((XC + 6,) + coarse, F32),
        pltpu.VMEM((XC + 4,) + flat, F32),
        pltpu.VMEM((XC + 4,) + coarse, F32),
        pltpu.VMEM((XC + 4,) + coarse, F32),
        pltpu.VMEM((XC + 4,) + coarse, F32),
        pltpu.VMEM((XC + 2,) + coarse, F32),
        pltpu.VMEM((XC + 2,) + coarse, F32),
        pltpu.VMEM((XC + 2,) + coarse, F32),
        pltpu.VMEM((XC + 2,) + coarse, F32),
        pltpu.VMEM((XC,) + flat, F32),
        pltpu.VMEM((2, TILES, 2, 8, 128), F32),
        pltpu.VMEM((MEMBERS, 2, 8, 128), F32),
        dma((5,)),
        dma((8,)),
        dma((8,)),
        dma((TILES,)),
        dma((TILES,)),
        dma((2, TILES)),
        dma((MEMBERS,)),
    ]
    return pl.pallas_call(
        kernel,
        out_shape=jax.ShapeDtypeStruct((4, 16, 32), F32),
        in_specs=[vmem, vmem, smem, smem, vmem, vmem, vmem, hbm, hbm],
        out_specs=vmem,
        scratch_shapes=scratch,
        compiler_params=pltpu.CompilerParams(
            collective_id=0, has_side_effects=True, vmem_limit_bytes=48 * 2**20
        ),
    )(*args)


def solution(mesh):
    return jax.shard_map(
        body,
        mesh=mesh,
        in_specs=(
            P("member", None),
            P("member", None),
            P("member"),
            P("member"),
            P(),
            P(),
            P(),
            P("tile", None, None),
            P(None, None, "tile"),
        ),
        out_specs=P("member", None, "tile"),
        check_vma=False,
    )
```

```python
import math

import jax
import jax.numpy as jnp
import numpy as np
from jax import lax
from jax.experimental import pallas as pl
from jax.experimental.pallas import tpu as pltpu
from jax.sharding import PartitionSpec as P

NODES = 9
SWEEPS = 3
CENTRE = 1.125
HALF_WIDTH = 0.875
SPREAD_RATIO = CENTRE / HALF_WIDTH
LOG2E = 1.0 / math.log(2.0)

F32 = jnp.float32
BF16 = jnp.bfloat16
MESH = pl.DeviceIdType.MESH

TILES = 8
MEMBERS = 16
KL = 12
KP = 16
XS = 16
XC = 8
XPAD = 8
OUTSIDE = -1024.0


def sweep_factors(sweep_count):
    previous = 1.0 / SPREAD_RATIO
    factors = []
    for _ in range(sweep_count - 1):
        current = 1.0 / (2.0 * SPREAD_RATIO - previous)
        factors.append((current * previous, 2.0 * current / HALF_WIDTH))
        previous = current
    return factors


(KEEP1, PUSH1), (KEEP2, PUSH2) = sweep_factors(SWEEPS)
FIRST = 1.0 / CENTRE
SHARE = (1.0 - FIRST) / FIRST
SECOND = PUSH1 * FIRST
BETA = KEEP1 / PUSH1 + SHARE
LEFT = (1.0 - PUSH1) * FIRST
A1 = FIRST + PUSH2 * (LEFT * (SHARE - BETA) - KEEP1 * FIRST)
A2 = (1.0 + KEEP2) * SECOND + PUSH2 * LEFT
A3 = PUSH2 * SECOND
R1 = A1 / A3
R2 = A2 / A3


def iota(shape, dim):
    return lax.broadcasted_iota(jnp.int32, shape, dim)


def halves(value):
    high = value.astype(BF16)
    return high, (value - high.astype(F32)).astype(BF16)


def thirds(value):
    high = value.astype(BF16)
    rest = value - high.astype(F32)
    middle = rest.astype(BF16)
    return high, middle, (rest - middle.astype(F32)).astype(BF16)


def cut(value, low, high, axis):
    return lax.slice_in_dim(value, low, high, axis=axis)


def faces(c, axis, roll_axis, size, first, last):
    n = c.shape[axis]
    head, tail = cut(c, 0, 1, axis), cut(c, n - 1, n, axis)
    wrap = tail + jnp.where(last, 0.0, pltpu.roll(head, size - 1, roll_axis))
    closed = jnp.where(last, 0.0, wrap)
    inner = cut(c, 0, n - 1, axis) + cut(c, 1, n, axis)
    down = jnp.where(first, head, pltpu.roll(closed, 1, roll_axis))
    up = jnp.concatenate([inner, wrap], axis)
    return jnp.concatenate([inner, closed], axis), up + jnp.concatenate([down, inner], axis)


def along(face, v, axis, roll_axis, size):
    n = v.shape[axis]
    inner, wrap = cut(face, 0, n - 1, axis), cut(face, n - 1, n, axis)
    up = jnp.concatenate(
        [inner * cut(v, 1, n, axis), wrap * pltpu.roll(cut(v, 0, 1, axis), size - 1, roll_axis)], axis
    )
    down = jnp.concatenate(
        [pltpu.roll(wrap * cut(v, n - 1, n, axis), 1, roll_axis), inner * cut(v, 0, n - 1, axis)], axis
    )
    return up + down


def pull(fx_low, fx_high, fy, fz, low, here, high):
    d = here.ndim
    across = fx_low * low + fx_high * high
    return (across + along(fy, here, d - 4, d - 1, 128)) + along(fz, here, d - 3, d - 2, 8)


def node_column(node_row):
    value = jnp.zeros(node_row.shape, F32)
    for node in range(NODES):
        value = jnp.where(
            node_row == node, math.cos(math.pi * node / (NODES - 1)) * LOG2E, value
        )
    spread = jnp.broadcast_to(value, (KP, KL))
    own = iota((KP, KL), 0) == iota((KP, KL), 1)
    return jnp.sum(jnp.where(own, spread, 0.0), axis=1, keepdims=True)


def block_transpose(blocks, width, lanes):
    count = len(blocks)
    place = lanes // width
    blocks = list(blocks)
    bit = 1
    while bit < count:
        clear = (place & bit) == 0
        for low in range(count):
            if low & bit:
                continue
            a, b = blocks[low], blocks[low | bit]
            blocks[low] = jnp.where(clear, a, pltpu.roll(b, width * bit, 1))
            blocks[low | bit] = jnp.where(clear, pltpu.roll(a, 128 - width * bit, 1), b)
        bit *= 2
    return blocks


def kernel(
    node_f,
    node_c,
    w_f,
    w_c,
    mode_x,
    mode_y,
    mode_z,
    src_f,
    src_c,
    perm_wide,
    perm_small,
    out,
    fraw,
    craw,
    cpack,
    cgot,
    nodes_f,
    nodes_c,
    weight_f,
    weight_c,
    mx,
    my_in,
    mz,
    mpad,
    xt,
    zt,
    perm_f,
    perm_c,
    rhs_f,
    rhs_c,
    c_f,
    c_c,
    inv_f,
    g_f,
    e_f,
    fx_f,
    fy_f,
    fz_f,
    fcoarse,
    inv_c,
    g_c,
    e_c,
    fx_c,
    fy_c,
    fz_c,
    tot,
    sendbuf,
    recvbuf,
    sumbuf,
    lastbuf,
    local_sem,
    halo_send,
    halo_recv,
    cs_send,
    cs_recv,
    fin_send,
    fin_recv,
    last_send,
    last_recv,
):
    me_m = lax.axis_index("member")
    me_t = lax.axis_index("tile")

    def to(member, tile):
        return {"member": member, "tile": tile}

    def bring(index, source, target):
        copy = pltpu.make_async_copy(source, target, local_sem.at[index])
        copy.start()
        return copy

    own_c = bring(0, src_c, craw)
    small = [
        bring(1, node_f, nodes_f),
        bring(2, node_c, nodes_c),
        bring(3, w_f, weight_f),
        bring(4, w_c, weight_c),
        bring(5, mode_x, mx),
        bring(6, mode_y, my_in),
        bring(7, mode_z, mz),
    ]
    perm = [bring(8, perm_wide, perm_f), bring(9, perm_small, perm_c)]
    own_f = [
        bring(10 + q, src_f.at[:, :, pl.ds(128 * q, 128)], fraw.at[pl.ds(2, XS), q])
        for q in range(4)
    ]

    barrier = pltpu.get_barrier_semaphore()
    for step in range(1, TILES):
        pl.semaphore_signal(
            barrier,
            inc=1,
            device_id=to(me_m, lax.rem(me_t + step, TILES)),
            device_id_type=MESH,
        )
    for step in range(1, MEMBERS):
        pl.semaphore_signal(
            barrier,
            inc=1,
            device_id=to(lax.rem(me_m + step, MEMBERS), me_t),
            device_id_type=MESH,
        )
    partner = to(2 * me_t + lax.rem(me_m, 2), me_m // 2)
    owns = me_m // 2 == me_t

    @pl.when(jnp.logical_not(owns))
    def _():
        pl.semaphore_signal(barrier, inc=1, device_id=partner, device_id_type=MESH)

    lanes = iota((8, 128), 1)
    subs = iota((8, 128), 0)
    masks = (lanes == 0, lanes == 127, subs == 0, subs == 7)

    own_c.wait()
    cpack[0:8] = jnp.zeros((8, 128), F32)
    cpack[264:272] = jnp.zeros((8, 128), F32)
    for quarter in range(4):
        rows = craw[4 * quarter : 4 * quarter + 4].reshape(128, 64)
        cpack[pl.ds(8 + quarter, 64, stride=4), :] = rows.T

    def interleave(parts):
        blocks = []
        for v in range(2):
            low = parts[0][:, 128 * v : 128 * v + 128]
            high = parts[1][:, 128 * v : 128 * v + 128]
            near = iota(low.shape, 1) < 64
            blocks.append(jnp.where(near, low, high))
            blocks.append(pltpu.roll(jnp.where(near, high, low), 64, 1))
        return jnp.concatenate(blocks, 1)

    for copy in small:
        copy.wait()
    for copy in perm:
        copy.wait()
    mpad[...] = jnp.zeros(mpad.shape, F32)
    mpad[0:KL, :] = my_in[...]
    parts = jnp.concatenate(thirds(mpad[...]), 0)
    my = 0.5 * interleave(
        [
            jnp.dot(
                parts[:, 256 * h : 256 * h + 256],
                perm_f[256 * h : 256 * h + 256, :],
                preferred_element_type=F32,
            )
            for h in range(2)
        ]
    )
    my = (my[0:KP] + my[KP : 2 * KP]) + my[2 * KP : 3 * KP]
    mpad[0:KL, 0:128] = mx[...]
    stacked = jnp.concatenate([mpad[:, 0:128]] * 8, 0)
    spare = jnp.where(iota((XPAD, 128), 1) == KL, 1.0, 0.0)
    xt[0:XPAD, :] = spare
    xt[XPAD : XPAD + 128, :] = stacked.T
    xt[XPAD + 128 : XPAD + 128 + XPAD, :] = spare
    mpad[0:KL, 0:32] = mz[...]
    stacked = jnp.concatenate([mpad[:, 0:32]] * 8, 0)
    zt[...] = jnp.where(iota((32, 128), 1) == KL, 1.0, stacked.T)
    zf = [zt[pl.ds(j, 8, stride=4), :] for j in range(4)]
    zc = [0.5 * (zf[2 * j] + zf[2 * j + 1]) for j in range(2)]
    zf = jnp.concatenate(zf, 0)
    zc = jnp.concatenate(zc, 0)

    def sides(value):
        high, low = halves(jnp.where(iota(value.shape, 0) == KL, OUTSIDE, value))
        return jnp.concatenate([high, low, high, low], 0)

    rhs_f[64:128, :] = jnp.zeros((64, 512), BF16)
    rhs_c[64:128, :] = jnp.zeros((64, 1024), BF16)
    rhs_f[0:64, :] = sides(my * node_column(nodes_f[...]))
    myc = jnp.concatenate(
        [
            0.5 * (my[:, 256 * k : 256 * k + 128] + my[:, 256 * k + 128 : 256 * k + 256])
            for k in range(2)
        ],
        1,
    )
    for m in range(4):
        rhs_c[0:64, 256 * m : 256 * m + 256] = sides(myc * node_column(nodes_c[m : m + 1, :]))

    def left(value):
        high = value.astype(BF16).astype(F32)
        return jnp.where(iota(value.shape, 1) < 32, high, value - high).astype(BF16)

    x0 = me_t * XS

    rows = []
    for i in range(XS + 6):
        rows.append(left(xt[pl.ds(x0 - 3 + XPAD + i, 1), :] * zf))
    logs = jnp.dot(jnp.concatenate(rows, 0), rhs_f[...], preferred_element_type=F32)
    for i in range(XS + 6):
        for k in range(4):
            for j in range(4):
                at = 32 * i + 8 * j
                c_f[i, k, j] = jnp.exp2(logs[at : at + 8, 128 * k : 128 * k + 128])

    pl.semaphore_wait(barrier, 23 - owns.astype(jnp.int32))

    has_left = me_t > 0
    has_right = me_t < TILES - 1

    def halo_copy(q, rightwards):
        if rightwards:
            return pltpu.make_async_remote_copy(
                src_ref=src_f.at[pl.ds(XS - 2, 2), :, pl.ds(128 * q, 128)],
                dst_ref=fraw.at[pl.ds(0, 2), q],
                send_sem=halo_send.at[q],
                recv_sem=halo_recv.at[q],
                device_id=to(me_m, lax.rem(me_t + 1, TILES)),
                device_id_type=MESH,
            )
        return pltpu.make_async_remote_copy(
            src_ref=src_f.at[pl.ds(0, 2), :, pl.ds(128 * q, 128)],
            dst_ref=fraw.at[pl.ds(XS + 2, 2), q],
            send_sem=halo_send.at[4 + q],
            recv_sem=halo_recv.at[4 + q],
            device_id=to(me_m, lax.rem(me_t + TILES - 1, TILES)),
            device_id_type=MESH,
        )

    @pl.when(has_right)
    def _():
        for q in range(4):
            halo_copy(q, True).start()

    @pl.when(has_left)
    def _():
        for q in range(4):
            halo_copy(q, False).start()

    @pl.when(jnp.logical_not(has_left))
    def _():
        fraw[0:2] = jnp.zeros((2, 4, 32, 128), F32)

    @pl.when(jnp.logical_not(has_right))
    def _():
        fraw[XS + 2 : XS + 4] = jnp.zeros((2, 4, 32, 128), F32)

    def strip_rows(tile):
        return cpack.at[pl.ds(pl.multiple_of(32 * tile, 8), 48)]

    def strip_copy(step):
        there = lax.rem(me_t + step, TILES)
        return pltpu.make_async_remote_copy(
            src_ref=strip_rows(there),
            dst_ref=cgot.at[me_t],
            send_sem=cs_send.at[step],
            recv_sem=cs_recv.at[step],
            device_id=to(me_m, there),
            device_id_type=MESH,
        )

    def set_up(planes, c, fx, fy, fz, inv):
        fx[0] = c[0] + c[1]

        def plane(n, carry):
            here = c[n + 1]
            d = here.ndim
            upper = here + c[n + 2]
            y_face, y_sum = faces(here, d - 4, d - 1, 128, masks[0], masks[1])
            z_face, z_sum = faces(here, d - 3, d - 2, 8, masks[2], masks[3])
            total = ((fx[n] + upper) + y_sum) + z_sum
            turned = pltpu.reciprocal(total, approx=True)
            turned = turned * (2.0 - total * turned)
            fx[n + 1] = upper
            fy[n] = y_face
            fz[n] = z_face
            inv[n] = turned
            return carry

        lax.fori_loop(0, planes, plane, 0)

        @pl.when(jnp.logical_not(has_left))
        def _():
            inv[0:2] = jnp.zeros((2,) + inv.shape[1:], F32)

        @pl.when(jnp.logical_not(has_right))
        def _():
            inv[planes - 2 : planes] = jnp.zeros((2,) + inv.shape[1:], F32)

    set_up(XS + 4, c_f, fx_f, fy_f, fz_f, inv_f)

    for step in range(1, TILES):
        strip_copy(step).start()
    cgot[me_t] = strip_rows(me_t)[...]

    rows = []
    for i in range(XC + 6):
        at = x0 - 6 + XPAD + 2 * i
        mean = 0.5 * (xt[pl.ds(at, 1), :] + xt[pl.ds(at + 1, 1), :])
        rows.append(left(mean * zc))
    logs = jnp.dot(jnp.concatenate(rows, 0), rhs_c[...], preferred_element_type=F32)
    for i in range(XC + 6):
        for m in range(4):
            for k in range(2):
                for j in range(2):
                    at, of = 16 * i + 8 * j, 256 * m + 128 * k
                    c_c[i, m, k, j] = jnp.exp2(logs[at : at + 8, of : of + 128])
    set_up(XC + 4, c_c, fx_c, fy_c, fz_c, inv_c)

    for copy in own_f:
        copy.wait()

    @pl.when(has_left)
    def _():
        for q in range(4):
            halo_copy(q, True).wait_recv()

    @pl.when(has_right)
    def _():
        for q in range(4):
            halo_copy(q, False).wait_recv()

    SOURCE_CHUNK = 10

    def source_fine(chunk, carry):
        halves_of_y = []
        for h in range(2):
            rows = []
            for i in range(SOURCE_CHUNK):
                for j in range(4):
                    rows.append(
                        jnp.concatenate(
                            [
                                fraw[SOURCE_CHUNK * chunk + i, 2 * h + q, pl.ds(j, 8, stride=4), :]
                                for q in range(2)
                            ],
                            1,
                        )
                    )
            high, low = halves(jnp.concatenate(rows, 0))
            order = perm_f[256 * h : 256 * h + 256, :]
            halves_of_y.append(
                jnp.dot(high, order, preferred_element_type=F32)
                + jnp.dot(low, order, preferred_element_type=F32)
            )
        got = interleave(halves_of_y)
        for i in range(SOURCE_CHUNK):
            n = SOURCE_CHUNK * chunk + i
            for k in range(4):
                for j in range(4):
                    at = 32 * i + 8 * j
                    g_f[n, k, j] = got[at : at + 8, 128 * k : 128 * k + 128] * inv_f[n, k, j]
        return carry

    lax.fori_loop(0, (XS + 4) // SOURCE_CHUNK, source_fine, 0)

    def sweep(planes, fx, fy, fz, inv, g, e):
        def plane(n, carry):
            here = g[n + 1]
            moved = pull(fx[n + 1], fx[n + 2], fy[n + 1], fz[n + 1], g[n], here, g[n + 2])
            e[n] = BETA * here + moved * inv[n + 1]
            return carry

        lax.fori_loop(0, planes, plane, 0)

    sweep(XS + 2, fx_f, fy_f, fz_f, inv_f, g_f, e_f)

    for step in range(1, TILES):
        strip_copy(step).wait_recv()
    rows = []
    for pair in range(6):
        at = slice(8 * pair, 8 * pair + 8)
        parts = [
            block_transpose([cgot[4 * half + q, at] for q in range(4)], 32, lanes)
            for half in range(2)
        ]
        for r in range(4):
            rows.append(jnp.concatenate([parts[0][r], parts[1][r]], 1))
    high, low = halves(jnp.concatenate(rows, 0))
    got = jnp.dot(high, perm_c[0:256, :], preferred_element_type=F32)
    got = got + jnp.dot(low, perm_c[0:256, :], preferred_element_type=F32)
    for pair in range(6):
        for r in range(4):
            for a in range(2):
                for k in range(2):
                    at = 32 * pair + 8 * r + 4 * a
                    fcoarse[2 * pair + a, k, r % 2, pl.ds(r // 2, 4, stride=2), :] = got[
                        at : at + 4, 128 * k : 128 * k + 128
                    ]
    for n in range(XC + 4):
        g_c[n] = fcoarse[n][None] * inv_c[n]
    sweep(XC + 2, fx_c, fy_c, fz_c, inv_c, g_c, e_c)

    scale_f = jnp.broadcast_to(weight_f[...].astype(F32) * (0.125 * A3), (8, 128))
    scale_c = [
        jnp.broadcast_to(weight_c[:, m : m + 1].astype(F32) * A3, (8, 128)) for m in range(4)
    ]

    def third(n, fx, fy, fz, inv, e):
        moved = pull(fx[n + 2], fx[n + 3], fy[n + 2], fz[n + 2], e[n], e[n + 1], e[n + 2])
        return moved * inv[n + 2]

    def block_sum(pair):
        rows = pair
        out_blocks = []
        for k in range(2):
            for j in range(2):
                out_blocks.append(
                    (rows[2 * k, 2 * j] + rows[2 * k + 1, 2 * j])
                    + (rows[2 * k, 2 * j + 1] + rows[2 * k + 1, 2 * j + 1])
                )
        return out_blocks

    def finish_plane(xc, carry):
        n = 2 * xc
        t_sum = block_sum(
            third(n, fx_f, fy_f, fz_f, inv_f, e_f) + third(n + 1, fx_f, fy_f, fz_f, inv_f, e_f)
        )
        g_sum = block_sum(g_f[n + 2] + g_f[n + 3])
        e_sum = block_sum(e_f[n + 1] + e_f[n + 2])
        coarse = (R1 * g_c[xc + 2] + R2 * e_c[xc + 1]) + third(
            xc, fx_c, fy_c, fz_c, inv_c, e_c
        )
        for k in range(2):
            for j in range(2):
                b = 2 * k + j
                block = scale_f * ((R1 * g_sum[b] + R2 * e_sum[b]) + t_sum[b])
                for m in range(4):
                    block = block + scale_c[m] * coarse[m, k, j]
                tot[xc, k, j] = block
        return carry

    def piece_copy(e, step):
        there = lax.rem(me_m // 2 + step, TILES)
        return pltpu.make_async_remote_copy(
            src_ref=sendbuf.at[e, there],
            dst_ref=recvbuf.at[lax.rem(me_m - 2 * there - e + 2 * MEMBERS, MEMBERS) - 1],
            send_sem=fin_send,
            recv_sem=fin_recv,
            device_id=to(2 * there + e, me_t),
            device_id_type=MESH,
        )

    for e in range(2):
        lax.fori_loop(4 * e, 4 * e + 4, finish_plane, 0)
        for chi in range(2):
            pieces = block_transpose(
                [
                    tot[4 * e + 2 * chi + a, k, j]
                    for a in range(2)
                    for j in range(2)
                    for k in range(2)
                ],
                16,
                lanes,
            )
            for t in range(TILES):
                sendbuf[e, t, 8 * chi : 8 * chi + 8, :] = pieces[t]
        for step in range(1, TILES):
            piece_copy(e, step).start()

        @pl.when(lax.rem(me_m, 2) != e)
        def _():
            piece_copy(e, 0).start()

    @pl.when(has_right)
    def _():
        for q in range(4):
            halo_copy(q, True).wait_send()

    @pl.when(has_left)
    def _():
        for q in range(4):
            halo_copy(q, False).wait_send()

    for step in range(1, TILES):
        strip_copy(step).wait_send()

    arrivals = pltpu.make_async_remote_copy(
        src_ref=recvbuf,
        dst_ref=recvbuf,
        send_sem=fin_send,
        recv_sem=fin_recv,
        device_id=to(lax.rem(me_m + 1, MEMBERS), me_t),
        device_id_type=MESH,
    )
    arrivals.wait_recv()
    terms = [sendbuf[lax.rem(me_m, 2), me_m // 2]] + [recvbuf[i] for i in range(MEMBERS - 1)]
    while len(terms) > 1:
        terms = [a + b for a, b in zip(terms[0::2], terms[1::2])]
    order = perm_c[256:384, 0:128]
    flat = sum(jnp.dot(part, order, preferred_element_type=F32) for part in thirds(terms[0]))
    last = pltpu.make_async_remote_copy(
        src_ref=sumbuf,
        dst_ref=lastbuf,
        send_sem=last_send,
        recv_sem=last_recv,
        device_id=partner,
        device_id_type=MESH,
    )
    sumbuf[...] = flat

    @pl.when(owns)
    def _():
        lastbuf[...] = sumbuf[...]

    @pl.when(jnp.logical_not(owns))
    def _():
        last.start()
        last.wait_recv()

    for chi in range(2):
        for g in range(4):
            out[2 * chi + g // 2, pl.ds(g % 2, 8, stride=2), :] = lastbuf[
                8 * chi : 8 * chi + 8, 32 * g : 32 * g + 32
            ]

    arrivals.wait_send()

    @pl.when(jnp.logical_not(owns))
    def _():
        last.wait_send()


def permutations():
    col = np.arange(256)
    wide = np.zeros((512, 256), np.float32)
    k = 2 * (col // 128) + (col % 128) // 64
    wide[4 * (col % 64) + k, col] = 2.0
    k = 2 * (col // 128) + 1 - (col % 128) // 64
    wide[256 + 4 * (col % 64) + k, col] = 2.0
    col = np.arange(256)
    small = np.zeros((384, 256), np.float32)
    small[2 * (col % 128) + col // 128, col] = 2.0
    row = np.arange(128)
    small[256 + row, (row & 96) + 2 * (row & 15) + ((row >> 4) & 1)] = 1.0
    return jnp.asarray(wide, BF16), jnp.asarray(small, BF16)


def body(
    node_fine,
    node_coarse,
    weight_fine,
    weight_coarse,
    mode_x,
    mode_y,
    mode_z,
    source_fine,
    source_coarse,
):
    hbm = pl.BlockSpec(memory_space=pl.ANY)
    fine = (4, 4, 8, 128)
    flat = (2, 2, 8, 128)
    coarse = (4, 2, 2, 8, 128)
    dma = pltpu.SemaphoreType.DMA

    def vmem(*shape, dtype=F32):
        return pltpu.VMEM(shape, dtype)

    scratch = [
        vmem(XS + 4, 4, 32, 128),
        vmem(16, 32, 64),
        vmem(272, 128),
        vmem(TILES, 48, 128),
        vmem(1, KL, dtype=jnp.int32),
        vmem(4, KL, dtype=jnp.int32),
        vmem(1, 1, dtype=jnp.int32),
        vmem(1, 4, dtype=jnp.int32),
        vmem(KL, 128),
        vmem(KL, 512),
        vmem(KL, 32),
        vmem(KP, 512),
        vmem(XPAD + 128 + XPAD, 128),
        vmem(32, 128),
        vmem(512, 256, dtype=BF16),
        vmem(384, 256, dtype=BF16),
        vmem(128, 512, dtype=BF16),
        vmem(128, 1024, dtype=BF16),
        vmem(XS + 6, *fine),
        vmem(XC + 6, *coarse),
        vmem(XS + 4, *fine),
        vmem(XS + 4, *fine),
        vmem(XS + 2, *fine),
        vmem(XS + 5, *fine),
        vmem(XS + 4, *fine),
        vmem(XS + 4, *fine),
        vmem(XC + 4, *flat),
        vmem(XC + 4, *coarse),
        vmem(XC + 4, *coarse),
        vmem(XC + 2, *coarse),
        vmem(XC + 5, *coarse),
        vmem(XC + 4, *coarse),
        vmem(XC + 4, *coarse),
        vmem(XC, *flat),
        vmem(2, TILES, 16, 128),
        vmem(MEMBERS - 1, 16, 128),
        vmem(16, 128),
        vmem(16, 128),
        dma((14,)),
        dma((8,)),
        dma((8,)),
        dma((TILES,)),
        dma((TILES,)),
        dma(()),
        dma(()),
        dma(()),
        dma(()),
    ]
    return pl.pallas_call(
        kernel,
        out_shape=jax.ShapeDtypeStruct((4, 16, 32), F32),
        in_specs=[hbm] * 11,
        out_specs=pl.BlockSpec(memory_space=pltpu.VMEM),
        scratch_shapes=scratch,
        compiler_params=pltpu.CompilerParams(
            collective_id=0, has_side_effects=True, vmem_limit_bytes=60 * 2**20
        ),
    )(
        node_fine,
        node_coarse,
        weight_fine.reshape(1, 1),
        weight_coarse.reshape(1, 4),
        mode_x,
        mode_y,
        mode_z,
        source_fine,
        jnp.transpose(source_coarse, (1, 2, 0)),
        *permutations(),
    )


def solution(mesh):
    return jax.shard_map(
        body,
        mesh=mesh,
        in_specs=(
            P("member", None),
            P("member", None),
            P("member"),
            P("member"),
            P(),
            P(),
            P(),
            P("tile", None, None),
            P(None, None, "tile"),
        ),
        out_specs=P("member", None, "tile"),
        check_vma=False,
    )
```

```python
import math

import jax
import jax.numpy as jnp
import numpy as np
from jax import lax
from jax.experimental import pallas as pl
from jax.experimental.pallas import tpu as pltpu
from jax.sharding import PartitionSpec as P

NODES = 9
SWEEPS = 3
CENTRE = 1.125
HALF_WIDTH = 0.875
SPREAD_RATIO = CENTRE / HALF_WIDTH
LOG2E = 1.0 / math.log(2.0)

F32 = jnp.float32
BF16 = jnp.bfloat16
MESH = pl.DeviceIdType.MESH

TILES = 8
MEMBERS = 16
KL = 12
KP = 16
XS = 16
XC = 8
XPAD = 8
OUTSIDE = -1024.0


def sweep_factors(sweep_count):
    previous = 1.0 / SPREAD_RATIO
    factors = []
    for _ in range(sweep_count - 1):
        current = 1.0 / (2.0 * SPREAD_RATIO - previous)
        factors.append((current * previous, 2.0 * current / HALF_WIDTH))
        previous = current
    return factors


(KEEP1, PUSH1), (KEEP2, PUSH2) = sweep_factors(SWEEPS)
FIRST = 1.0 / CENTRE
SHARE = (1.0 - FIRST) / FIRST
SECOND = PUSH1 * FIRST
BETA = KEEP1 / PUSH1 + SHARE
LEFT = (1.0 - PUSH1) * FIRST
A1 = FIRST + PUSH2 * (LEFT * (SHARE - BETA) - KEEP1 * FIRST)
A2 = (1.0 + KEEP2) * SECOND + PUSH2 * LEFT
A3 = PUSH2 * SECOND
R1 = A1 / A3
R2 = A2 / A3


def iota(shape, dim):
    return lax.broadcasted_iota(jnp.int32, shape, dim)


def halves(value):
    high = value.astype(BF16)
    return high, (value - high.astype(F32)).astype(BF16)


def thirds(value):
    high = value.astype(BF16)
    rest = value - high.astype(F32)
    middle = rest.astype(BF16)
    return high, middle, (rest - middle.astype(F32)).astype(BF16)


def cut(value, low, high, axis):
    return lax.slice_in_dim(value, low, high, axis=axis)


def faces(c, axis, roll_axis, size, first, last):
    n = c.shape[axis]
    head, tail = cut(c, 0, 1, axis), cut(c, n - 1, n, axis)
    wrap = tail + jnp.where(last, 0.0, pltpu.roll(head, size - 1, roll_axis))
    closed = jnp.where(last, 0.0, wrap)
    inner = cut(c, 0, n - 1, axis) + cut(c, 1, n, axis)
    down = jnp.where(first, head, pltpu.roll(closed, 1, roll_axis))
    up = jnp.concatenate([inner, wrap], axis)
    return jnp.concatenate([inner, closed], axis), up + jnp.concatenate([down, inner], axis)


def along(face, v, axis, roll_axis, size):
    n = v.shape[axis]
    inner, wrap = cut(face, 0, n - 1, axis), cut(face, n - 1, n, axis)
    up = jnp.concatenate(
        [inner * cut(v, 1, n, axis), wrap * pltpu.roll(cut(v, 0, 1, axis), size - 1, roll_axis)], axis
    )
    down = jnp.concatenate(
        [pltpu.roll(wrap * cut(v, n - 1, n, axis), 1, roll_axis), inner * cut(v, 0, n - 1, axis)], axis
    )
    return up + down


def pull(fx_low, fx_high, fy, fz, low, here, high):
    d = here.ndim
    across = fx_low * low + fx_high * high
    return (across + along(fy, here, d - 4, d - 1, 128)) + along(fz, here, d - 3, d - 2, 8)


def node_column(node_row):
    value = jnp.zeros(node_row.shape, F32)
    for node in range(NODES):
        value = jnp.where(
            node_row == node, math.cos(math.pi * node / (NODES - 1)) * LOG2E, value
        )
    spread = jnp.broadcast_to(value, (KP, KL))
    own = iota((KP, KL), 0) == iota((KP, KL), 1)
    return jnp.sum(jnp.where(own, spread, 0.0), axis=1, keepdims=True)


def block_transpose(blocks, width, lanes):
    count = len(blocks)
    place = lanes // width
    blocks = list(blocks)
    bit = 1
    while bit < count:
        clear = (place & bit) == 0
        for low in range(count):
            if low & bit:
                continue
            a, b = blocks[low], blocks[low | bit]
            blocks[low] = jnp.where(clear, a, pltpu.roll(b, width * bit, 1))
            blocks[low | bit] = jnp.where(clear, pltpu.roll(a, 128 - width * bit, 1), b)
        bit *= 2
    return blocks


def kernel(
    node_f,
    node_c,
    w_f,
    w_c,
    mode_x,
    mode_y,
    mode_z,
    src_f,
    src_c,
    perm_wide,
    perm_small,
    out,
    fraw,
    craw,
    cpack,
    cgot,
    nodes_f,
    nodes_c,
    weight_f,
    weight_c,
    mx,
    my_in,
    mz,
    mpad,
    xt,
    zt,
    perm_f,
    perm_c,
    rhs_f,
    rhs_c,
    c_f,
    c_c,
    inv_f,
    g_f,
    e_f,
    fx_f,
    fy_f,
    fz_f,
    fcoarse,
    inv_c,
    g_c,
    e_c,
    fx_c,
    fy_c,
    fz_c,
    tot,
    sendbuf,
    sharebuf,
    outbuf,
    recvbuf,
    local_sem,
    halo_send,
    halo_recv,
    cs_send,
    cs_recv,
    fwd_send,
    fwd_recv,
    fin_send,
    fin_recv,
):
    me_m = lax.axis_index("member")
    me_t = lax.axis_index("tile")

    def to(member, tile):
        return {"member": member, "tile": tile}

    def bring(index, source, target):
        copy = pltpu.make_async_copy(source, target, local_sem.at[index])
        copy.start()
        return copy

    small = [
        bring(1, node_f, nodes_f),
        bring(2, node_c, nodes_c),
        bring(3, w_f, weight_f),
        bring(4, w_c, weight_c),
        bring(5, mode_x, mx),
        bring(6, mode_y, my_in),
        bring(7, mode_z, mz),
    ]
    own_c = bring(0, src_c, craw)
    perm = [bring(8, perm_wide, perm_f), bring(9, perm_small, perm_c)]
    own_f = [
        bring(10 + q, src_f.at[:, :, pl.ds(128 * q, 128)], fraw.at[pl.ds(2, XS), q])
        for q in range(4)
    ]

    barrier = pltpu.get_barrier_semaphore()
    for step in range(1, TILES):
        pl.semaphore_signal(
            barrier,
            inc=1,
            device_id=to(me_m, lax.rem(me_t + step, TILES)),
            device_id_type=MESH,
        )
    core = lax.rem(me_m, 2)
    sibling = to(me_m + 1 - 2 * core, me_t)
    pl.semaphore_signal(barrier, inc=1, device_id=sibling, device_id_type=MESH)
    feeding_tile = me_m // 2
    for step in range(2, MEMBERS, 2):
        pl.semaphore_signal(
            barrier,
            inc=1,
            device_id=to(lax.rem(me_m + step, MEMBERS), feeding_tile),
            device_id_type=MESH,
        )
    feeds_itself = feeding_tile == me_t

    lanes = iota((8, 128), 1)
    subs = iota((8, 128), 0)
    masks = (lanes == 0, lanes == 127, subs == 0, subs == 7)

    own_c.wait()
    cpack[0:8] = jnp.zeros((8, 128), F32)
    cpack[264:272] = jnp.zeros((8, 128), F32)
    for quarter in range(4):
        rows = craw[4 * quarter : 4 * quarter + 4].reshape(128, 64)
        cpack[pl.ds(8 + quarter, 64, stride=4), :] = rows.T

    pl.semaphore_wait(barrier, 16 - 8 * feeds_itself.astype(jnp.int32))

    has_left = me_t > 0
    has_right = me_t < TILES - 1

    def halo_copy(q, rightwards):
        here = pl.ds(pl.multiple_of(256 * core + 128 * q, 128), 128)
        if rightwards:
            return pltpu.make_async_remote_copy(
                src_ref=src_f.at[pl.ds(XS - 2, 2), :, here],
                dst_ref=fraw.at[pl.ds(0, 2), 2 * core + q],
                send_sem=halo_send.at[q],
                recv_sem=halo_recv.at[q],
                device_id=to(me_m, lax.rem(me_t + 1, TILES)),
                device_id_type=MESH,
            )
        return pltpu.make_async_remote_copy(
            src_ref=src_f.at[pl.ds(0, 2), :, here],
            dst_ref=fraw.at[pl.ds(XS + 2, 2), 2 * core + q],
            send_sem=halo_send.at[2 + q],
            recv_sem=halo_recv.at[2 + q],
            device_id=to(me_m, lax.rem(me_t + TILES - 1, TILES)),
            device_id_type=MESH,
        )

    def hand_over(index, part):
        return pltpu.make_async_remote_copy(
            src_ref=part,
            dst_ref=part,
            send_sem=fwd_send.at[index],
            recv_sem=fwd_recv.at[index],
            device_id=sibling,
            device_id_type=MESH,
        )

    halo_over = [
        hand_over(0, fraw.at[pl.ds(0, 2), pl.ds(2 * core, 2)]),
        hand_over(1, fraw.at[pl.ds(XS + 2, 2), pl.ds(2 * core, 2)]),
    ]
    own_rows = pl.ds(pl.multiple_of(24 * core, 8), 24)
    strip_over = hand_over(2, cgot.at[:, own_rows])

    @pl.when(has_right)
    def _():
        for q in range(2):
            halo_copy(q, True).start()

    @pl.when(has_left)
    def _():
        for q in range(2):
            halo_copy(q, False).start()

    @pl.when(jnp.logical_not(has_left))
    def _():
        fraw[0:2] = jnp.zeros((2, 4, 32, 128), F32)

    @pl.when(jnp.logical_not(has_right))
    def _():
        fraw[XS + 2 : XS + 4] = jnp.zeros((2, 4, 32, 128), F32)

    def interleave(parts):
        blocks = []
        for v in range(2):
            low = parts[0][:, 128 * v : 128 * v + 128]
            high = parts[1][:, 128 * v : 128 * v + 128]
            near = iota(low.shape, 1) < 64
            blocks.append(jnp.where(near, low, high))
            blocks.append(pltpu.roll(jnp.where(near, high, low), 64, 1))
        return jnp.concatenate(blocks, 1)

    for copy in small:
        copy.wait()
    for copy in perm:
        copy.wait()
    mpad[...] = jnp.zeros(mpad.shape, F32)
    mpad[0:KL, :] = my_in[...]
    parts = jnp.concatenate(thirds(mpad[...]), 0)
    my = 0.5 * interleave(
        [
            jnp.dot(
                parts[:, 256 * h : 256 * h + 256],
                perm_f[256 * h : 256 * h + 256, :],
                preferred_element_type=F32,
            )
            for h in range(2)
        ]
    )
    my = (my[0:KP] + my[KP : 2 * KP]) + my[2 * KP : 3 * KP]
    mpad[0:KL, 0:128] = mx[...]
    stacked = jnp.concatenate([mpad[:, 0:128]] * 8, 0)
    spare = jnp.where(iota((XPAD, 128), 1) == KL, 1.0, 0.0)
    xt[0:XPAD, :] = spare
    xt[XPAD : XPAD + 128, :] = stacked.T
    xt[XPAD + 128 : XPAD + 128 + XPAD, :] = spare
    mpad[0:KL, 0:32] = mz[...]
    stacked = jnp.concatenate([mpad[:, 0:32]] * 8, 0)
    zt[...] = jnp.where(iota((32, 128), 1) == KL, 1.0, stacked.T)
    zf = [zt[pl.ds(j, 8, stride=4), :] for j in range(4)]
    zc = [0.5 * (zf[2 * j] + zf[2 * j + 1]) for j in range(2)]
    zf = jnp.concatenate(zf, 0)
    zc = jnp.concatenate(zc, 0)

    def sides(value):
        high, low = halves(jnp.where(iota(value.shape, 0) == KL, OUTSIDE, value))
        return jnp.concatenate([high, low, high, low], 0)

    rhs_f[64:128, :] = jnp.zeros((64, 512), BF16)
    rhs_c[64:128, :] = jnp.zeros((64, 1024), BF16)
    rhs_f[0:64, :] = sides(my * node_column(nodes_f[...]))
    myc = jnp.concatenate(
        [
            0.5 * (my[:, 256 * k : 256 * k + 128] + my[:, 256 * k + 128 : 256 * k + 256])
            for k in range(2)
        ],
        1,
    )
    for m in range(4):
        rhs_c[0:64, 256 * m : 256 * m + 256] = sides(myc * node_column(nodes_c[m : m + 1, :]))

    def left(value):
        high = value.astype(BF16).astype(F32)
        return jnp.where(iota(value.shape, 1) < 32, high, value - high).astype(BF16)

    x0 = me_t * XS

    rows = []
    for i in range(XS + 6):
        rows.append(left(xt[pl.ds(x0 - 3 + XPAD + i, 1), :] * zf))
    logs = jnp.dot(jnp.concatenate(rows, 0), rhs_f[...], preferred_element_type=F32)
    for i in range(XS + 6):
        for k in range(4):
            for j in range(4):
                at = 32 * i + 8 * j
                c_f[i, k, j] = jnp.exp2(logs[at : at + 8, 128 * k : 128 * k + 128])

    def strip_rows(tile):
        return cpack.at[pl.ds(pl.multiple_of(32 * tile + 24 * core, 8), 24)]

    def strip_copy(step):
        there = lax.rem(me_t + step, TILES)
        return pltpu.make_async_remote_copy(
            src_ref=strip_rows(there),
            dst_ref=cgot.at[me_t, own_rows],
            send_sem=cs_send.at[step],
            recv_sem=cs_recv.at[step],
            device_id=to(me_m, there),
            device_id_type=MESH,
        )

    for step in range(1, TILES):
        strip_copy(step).start()
    cgot[me_t, own_rows] = strip_rows(me_t)[...]

    def set_up(planes, c, fx, fy, fz, inv):
        fx[0] = c[0] + c[1]

        def plane(n, carry):
            here = c[n + 1]
            d = here.ndim
            upper = here + c[n + 2]
            y_face, y_sum = faces(here, d - 4, d - 1, 128, masks[0], masks[1])
            z_face, z_sum = faces(here, d - 3, d - 2, 8, masks[2], masks[3])
            total = ((fx[n] + upper) + y_sum) + z_sum
            turned = pltpu.reciprocal(total, approx=True)
            fx[n + 1] = upper
            fy[n] = y_face
            fz[n] = z_face
            inv[n] = turned
            return carry

        lax.fori_loop(0, planes, plane, 0, unroll=4 if planes == XS + 4 else 4)

        @pl.when(jnp.logical_not(has_left))
        def _():
            inv[0:2] = jnp.zeros((2,) + inv.shape[1:], F32)

        @pl.when(jnp.logical_not(has_right))
        def _():
            inv[planes - 2 : planes] = jnp.zeros((2,) + inv.shape[1:], F32)

    set_up(XS + 4, c_f, fx_f, fy_f, fz_f, inv_f)

    @pl.when(has_left)
    def _():
        for q in range(2):
            halo_copy(q, True).wait_recv()
        halo_over[0].start()

    @pl.when(has_right)
    def _():
        for q in range(2):
            halo_copy(q, False).wait_recv()
        halo_over[1].start()


    rows = []
    for i in range(XC + 6):
        at = x0 - 6 + XPAD + 2 * i
        mean = 0.5 * (xt[pl.ds(at, 1), :] + xt[pl.ds(at + 1, 1), :])
        rows.append(left(mean * zc))
    logs = jnp.dot(jnp.concatenate(rows, 0), rhs_c[...], preferred_element_type=F32)
    for i in range(XC + 6):
        for m in range(4):
            for k in range(2):
                for j in range(2):
                    at, of = 16 * i + 8 * j, 256 * m + 128 * k
                    c_c[i, m, k, j] = jnp.exp2(logs[at : at + 8, of : of + 128])
    set_up(XC + 4, c_c, fx_c, fy_c, fz_c, inv_c)

    for step in range(1, TILES):
        strip_copy(step).wait_recv()
    strip_over.start()

    for copy in own_f:
        copy.wait()

    @pl.when(has_left)
    def _():
        halo_over[0].wait_recv()

    @pl.when(has_right)
    def _():
        halo_over[1].wait_recv()

    SOURCE_CHUNK = 10

    def source_fine(chunk, carry):
        halves_of_y = []
        for h in range(2):
            rows = []
            for i in range(SOURCE_CHUNK):
                for j in range(4):
                    rows.append(
                        jnp.concatenate(
                            [
                                fraw[SOURCE_CHUNK * chunk + i, 2 * h + q, pl.ds(j, 8, stride=4), :]
                                for q in range(2)
                            ],
                            1,
                        )
                    )
            high, low = halves(jnp.concatenate(rows, 0))
            order = perm_f[256 * h : 256 * h + 256, :]
            halves_of_y.append(
                jnp.dot(high, order, preferred_element_type=F32)
                + jnp.dot(low, order, preferred_element_type=F32)
            )
        got = interleave(halves_of_y)
        for i in range(SOURCE_CHUNK):
            n = SOURCE_CHUNK * chunk + i
            for k in range(4):
                for j in range(4):
                    at = 32 * i + 8 * j
                    g_f[n, k, j] = got[at : at + 8, 128 * k : 128 * k + 128] * inv_f[n, k, j]
        return carry

    lax.fori_loop(0, (XS + 4) // SOURCE_CHUNK, source_fine, 0)

    def sweep(planes, fx, fy, fz, inv, g, e):
        def plane(n, carry):
            here = g[n + 1]
            moved = pull(fx[n + 1], fx[n + 2], fy[n + 1], fz[n + 1], g[n], here, g[n + 2])
            e[n] = BETA * here + moved * inv[n + 1]
            return carry

        lax.fori_loop(0, planes, plane, 0, unroll=3 if planes == XS + 2 else 5)

    sweep(XS + 2, fx_f, fy_f, fz_f, inv_f, g_f, e_f)

    strip_over.wait_recv()
    rows = []
    for pair in range(6):
        at = slice(8 * pair, 8 * pair + 8)
        parts = [
            block_transpose([cgot[4 * half + q, at] for q in range(4)], 32, lanes)
            for half in range(2)
        ]
        for r in range(4):
            rows.append(jnp.concatenate([parts[0][r], parts[1][r]], 1))
    high, low = halves(jnp.concatenate(rows, 0))
    got = jnp.dot(high, perm_c[0:256, :], preferred_element_type=F32)
    got = got + jnp.dot(low, perm_c[0:256, :], preferred_element_type=F32)
    for pair in range(6):
        for r in range(4):
            for a in range(2):
                for k in range(2):
                    at = 32 * pair + 8 * r + 4 * a
                    fcoarse[2 * pair + a, k, r % 2, pl.ds(r // 2, 4, stride=2), :] = got[
                        at : at + 4, 128 * k : 128 * k + 128
                    ]
    for n in range(XC + 4):
        g_c[n] = fcoarse[n][None] * inv_c[n]
    sweep(XC + 2, fx_c, fy_c, fz_c, inv_c, g_c, e_c)

    scale_f = jnp.broadcast_to(weight_f[...].astype(F32) * (0.125 * A3), (8, 128))
    scale_c = [
        jnp.broadcast_to(weight_c[:, m : m + 1].astype(F32) * A3, (8, 128)) for m in range(4)
    ]

    def third(n, fx, fy, fz, inv, e):
        moved = pull(fx[n + 2], fx[n + 3], fy[n + 2], fz[n + 2], e[n], e[n + 1], e[n + 2])
        return moved * inv[n + 2]

    def block_sum(pair):
        rows = pair
        out_blocks = []
        for k in range(2):
            for j in range(2):
                out_blocks.append(
                    (rows[2 * k, 2 * j] + rows[2 * k + 1, 2 * j])
                    + (rows[2 * k, 2 * j + 1] + rows[2 * k + 1, 2 * j + 1])
                )
        return out_blocks

    def finish_plane(xc, carry):
        n = 2 * xc
        t_sum = block_sum(
            third(n, fx_f, fy_f, fz_f, inv_f, e_f) + third(n + 1, fx_f, fy_f, fz_f, inv_f, e_f)
        )
        g_sum = block_sum(g_f[n + 2] + g_f[n + 3])
        e_sum = block_sum(e_f[n + 1] + e_f[n + 2])
        coarse = (R1 * g_c[xc + 2] + R2 * e_c[xc + 1]) + third(
            xc, fx_c, fy_c, fz_c, inv_c, e_c
        )
        for k in range(2):
            for j in range(2):
                b = 2 * k + j
                block = scale_f * ((R1 * g_sum[b] + R2 * e_sum[b]) + t_sum[b])
                for m in range(4):
                    block = block + scale_c[m] * coarse[m, k, j]
                tot[xc, k, j] = block
        return carry

    def pieces_of(first):
        return block_transpose(
            [tot[first + a, k, j] for a in range(2) for j in range(2) for k in range(2)],
            16,
            lanes,
        )

    def finish_planes(first, count):
        def one(i, carry):
            return finish_plane(first + i, carry)

        lax.fori_loop(0, count, one, 0, unroll=2)

    other = 1 - core
    finish_planes(4 * other, 4)
    for chi in range(2):
        pieces = pieces_of(4 * other + 2 * chi)
        for t in range(TILES):
            sendbuf[chi, t] = pieces[t]
    share = pltpu.make_async_remote_copy(
        src_ref=sendbuf,
        dst_ref=sharebuf,
        send_sem=fwd_send.at[3],
        recv_sem=fwd_recv.at[3],
        device_id=sibling,
        device_id_type=MESH,
    )
    share.start()

    def piece_copy(chi, step):
        there = lax.rem(me_t + step, TILES)
        return pltpu.make_async_remote_copy(
            src_ref=outbuf.at[chi, there],
            dst_ref=recvbuf.at[me_m // 2, chi],
            send_sem=fin_send,
            recv_sem=fin_recv,
            device_id=to(2 * me_t + core, there),
            device_id_type=MESH,
        )

    for chi in range(2):
        finish_planes(4 * core + 2 * chi, 2)
        if chi == 0:
            share.wait_recv()
        pieces = pieces_of(4 * core + 2 * chi)
        for t in range(TILES):
            outbuf[chi, t] = pieces[t] + sharebuf[chi, t]
        for step in range(1, TILES):
            piece_copy(chi, step).start()

        @pl.when(feeds_itself)
        def _():
            recvbuf[me_m // 2, chi] = outbuf[chi, me_t]

        @pl.when(jnp.logical_not(feeds_itself))
        def _():
            piece_copy(chi, 0).start()

    @pl.when(has_right)
    def _():
        for q in range(2):
            halo_copy(q, True).wait_send()
        halo_over[1].wait_send()

    @pl.when(has_left)
    def _():
        for q in range(2):
            halo_copy(q, False).wait_send()
        halo_over[0].wait_send()

    for step in range(1, TILES):
        strip_copy(step).wait_send()
    strip_over.wait_send()
    share.wait_send()

    def arrivals(count):
        return pltpu.make_async_remote_copy(
            src_ref=recvbuf.at[pl.ds(0, count)],
            dst_ref=recvbuf.at[pl.ds(0, count)],
            send_sem=fin_send,
            recv_sem=fin_recv,
            device_id=to(me_m, lax.rem(me_t + 1, TILES)),
            device_id_type=MESH,
        )

    @pl.when(feeds_itself)
    def _():
        arrivals(TILES - 1).wait_recv()

    @pl.when(jnp.logical_not(feeds_itself))
    def _():
        arrivals(TILES).wait_recv()

    terms = [recvbuf[i].reshape(16, 128) for i in range(TILES)]
    while len(terms) > 1:
        terms = [a + b for a, b in zip(terms[0::2], terms[1::2])]
    order = perm_c[256:384, 0:128]
    flat = sum(jnp.dot(part, order, preferred_element_type=F32) for part in thirds(terms[0]))
    for chi in range(2):
        for g in range(4):
            out[2 * chi + g // 2, pl.ds(g % 2, 8, stride=2), :] = flat[
                8 * chi : 8 * chi + 8, 32 * g : 32 * g + 32
            ]

    @pl.when(feeds_itself)
    def _():
        arrivals(TILES - 1).wait_send()

    @pl.when(jnp.logical_not(feeds_itself))
    def _():
        arrivals(TILES).wait_send()


def permutations():
    col = np.arange(256)
    wide = np.zeros((512, 256), np.float32)
    k = 2 * (col // 128) + (col % 128) // 64
    wide[4 * (col % 64) + k, col] = 2.0
    k = 2 * (col // 128) + 1 - (col % 128) // 64
    wide[256 + 4 * (col % 64) + k, col] = 2.0
    col = np.arange(256)
    small = np.zeros((384, 256), np.float32)
    small[2 * (col % 128) + col // 128, col] = 2.0
    row = np.arange(128)
    small[256 + row, (row & 96) + 2 * (row & 15) + ((row >> 4) & 1)] = 1.0
    return jnp.asarray(wide, BF16), jnp.asarray(small, BF16)


def body(
    node_fine,
    node_coarse,
    weight_fine,
    weight_coarse,
    mode_x,
    mode_y,
    mode_z,
    source_fine,
    source_coarse,
):
    hbm = pl.BlockSpec(memory_space=pl.ANY)
    fine = (4, 4, 8, 128)
    flat = (2, 2, 8, 128)
    coarse = (4, 2, 2, 8, 128)
    dma = pltpu.SemaphoreType.DMA

    def vmem(*shape, dtype=F32):
        return pltpu.VMEM(shape, dtype)

    scratch = [
        vmem(XS + 4, 4, 32, 128),
        vmem(16, 32, 64),
        vmem(272, 128),
        vmem(TILES, 48, 128),
        vmem(1, KL, dtype=jnp.int32),
        vmem(4, KL, dtype=jnp.int32),
        vmem(1, 1, dtype=jnp.int32),
        vmem(1, 4, dtype=jnp.int32),
        vmem(KL, 128),
        vmem(KL, 512),
        vmem(KL, 32),
        vmem(KP, 512),
        vmem(XPAD + 128 + XPAD, 128),
        vmem(32, 128),
        vmem(512, 256, dtype=BF16),
        vmem(384, 256, dtype=BF16),
        vmem(128, 512, dtype=BF16),
        vmem(128, 1024, dtype=BF16),
        vmem(XS + 6, *fine),
        vmem(XC + 6, *coarse),
        vmem(XS + 4, *fine),
        vmem(XS + 4, *fine),
        vmem(XS + 2, *fine),
        vmem(XS + 5, *fine),
        vmem(XS + 4, *fine),
        vmem(XS + 4, *fine),
        vmem(XC + 4, *flat),
        vmem(XC + 4, *coarse),
        vmem(XC + 4, *coarse),
        vmem(XC + 2, *coarse),
        vmem(XC + 5, *coarse),
        vmem(XC + 4, *coarse),
        vmem(XC + 4, *coarse),
        vmem(XC, *flat),
        vmem(2, TILES, 8, 128),
        vmem(2, TILES, 8, 128),
        vmem(2, TILES, 8, 128),
        vmem(TILES, 2, 8, 128),
        dma((14,)),
        dma((4,)),
        dma((4,)),
        dma((TILES,)),
        dma((TILES,)),
        dma((4,)),
        dma((4,)),
        dma(()),
        dma(()),
    ]
    return pl.pallas_call(
        kernel,
        out_shape=jax.ShapeDtypeStruct((4, 16, 32), F32),
        in_specs=[hbm] * 11,
        out_specs=pl.BlockSpec(memory_space=pltpu.VMEM),
        scratch_shapes=scratch,
        compiler_params=pltpu.CompilerParams(
            collective_id=0, has_side_effects=True, vmem_limit_bytes=60 * 2**20
        ),
    )(
        node_fine,
        node_coarse,
        weight_fine.reshape(1, 1),
        weight_coarse.reshape(1, 4),
        mode_x,
        mode_y,
        mode_z,
        source_fine,
        jnp.transpose(source_coarse, (1, 2, 0)),
        *permutations(),
    )


def solution(mesh):
    return jax.shard_map(
        body,
        mesh=mesh,
        in_specs=(
            P("member", None),
            P("member", None),
            P("member"),
            P("member"),
            P(),
            P(),
            P(),
            P("tile", None, None),
            P(None, None, "tile"),
        ),
        out_specs=P("member", None, "tile"),
        check_vma=False,
    )
```

```python
import math

import jax
import jax.numpy as jnp
import numpy as np
from jax import lax
from jax.experimental import pallas as pl
from jax.experimental.pallas import tpu as pltpu
from jax.sharding import PartitionSpec as P

NODES = 9
SWEEPS = 3
CENTRE = 1.125
HALF_WIDTH = 0.875
SPREAD_RATIO = CENTRE / HALF_WIDTH
LOG2E = 1.0 / math.log(2.0)

F32 = jnp.float32
BF16 = jnp.bfloat16
MESH = pl.DeviceIdType.MESH

TILES = 8
MEMBERS = 16
KL = 12
KP = 16
XF = 8
XC = 4
KF = 9
KC = 5
XPAD = 8
OUTSIDE = -1024.0


def sweep_factors(sweep_count):
    previous = 1.0 / SPREAD_RATIO
    factors = []
    for _ in range(sweep_count - 1):
        current = 1.0 / (2.0 * SPREAD_RATIO - previous)
        factors.append((current * previous, 2.0 * current / HALF_WIDTH))
        previous = current
    return factors


(KEEP1, PUSH1), (KEEP2, PUSH2) = sweep_factors(SWEEPS)
FIRST = 1.0 / CENTRE
SHARE = (1.0 - FIRST) / FIRST
SECOND = PUSH1 * FIRST
BETA = KEEP1 / PUSH1 + SHARE
LEFT = (1.0 - PUSH1) * FIRST
A1 = FIRST + PUSH2 * (LEFT * (SHARE - BETA) - KEEP1 * FIRST)
A2 = (1.0 + KEEP2) * SECOND + PUSH2 * LEFT
A3 = PUSH2 * SECOND
R1 = A1 / A3
R2 = A2 / A3


def iota(shape, dim):
    return lax.broadcasted_iota(jnp.int32, shape, dim)


def halves(value):
    high = value.astype(BF16)
    return high, (value - high.astype(F32)).astype(BF16)


def thirds(value):
    high = value.astype(BF16)
    rest = value - high.astype(F32)
    middle = rest.astype(BF16)
    return high, middle, (rest - middle.astype(F32)).astype(BF16)


def cut(value, low, high, axis):
    return lax.slice_in_dim(value, low, high, axis=axis)


def node_values(index):
    value = jnp.zeros(index.shape, F32)
    for node in range(NODES):
        value = jnp.where(index == node, math.cos(math.pi * node / (NODES - 1)) * LOG2E, value)
    return value


def z_faces(c, masks):
    n = c.shape[0]
    wrap = c[n - 1 : n] + jnp.where(masks[3], 0.0, pltpu.roll(c[0:1], 7, 1))
    closed = jnp.where(masks[3], 0.0, wrap)
    inner = c[0 : n - 1] + c[1:n]
    down = jnp.where(masks[2], c[0:1], pltpu.roll(closed, 1, 1))
    up = jnp.concatenate([inner, wrap], 0)
    return jnp.concatenate([inner, closed], 0), up + jnp.concatenate([down, inner], 0)


def z_pull(face, v):
    n = v.shape[0]
    inner, wrap = face[0 : n - 1], face[n - 1 : n]
    up = jnp.concatenate([inner * v[1:n], wrap * pltpu.roll(v[0:1], 7, 1)], 0)
    down = jnp.concatenate([pltpu.roll(wrap * v[n - 1 : n], 1, 1), inner * v[0 : n - 1]], 0)
    return up + down


class Level:
    def __init__(self, ks, c, fx, fy, fz, inv, g, e):
        self.ks, self.c, self.fx, self.fy, self.fz = ks, c, fx, fy, fz
        self.inv, self.g, self.e = inv, g, e

    def set_up(self, n, rest, masks, hide):
        ks = self.ks
        c = [self.c[(n + 1,) + rest + (k,)] for k in range(ks)]
        wrap = c[ks - 1] + jnp.where(masks[1], 0.0, pltpu.roll(c[0], 127, 2))
        closed = jnp.where(masks[1], 0.0, wrap)
        down = jnp.where(masks[0], c[0], pltpu.roll(closed, 1, 2))
        for k in range(ks):
            upper = c[k] + self.c[(n + 2,) + rest + (k,)]
            next_face = c[k] + c[k + 1] if k < ks - 1 else wrap
            z_face, z_sum = z_faces(c[k], masks)
            total = ((self.fx[(n,) + rest + (k,)] + upper) + (next_face + down)) + z_sum
            turned = pltpu.reciprocal(total, approx=True)
            for mask in hide(k):
                turned = jnp.where(mask, 0.0, turned)
            self.fx[(n + 1,) + rest + (k,)] = upper
            self.fy[(n,) + rest + (k,)] = next_face if k < ks - 1 else closed
            self.fz[(n,) + rest + (k,)] = z_face
            self.inv[(n,) + rest + (k,)] = turned
            down = next_face

    def pull(self, v, n, shift, rest):
        ks = self.ks
        f = n + shift
        last = v[(n,) + rest + (ks - 1,)]
        wrap = self.fy[(f,) + rest + (ks - 1,)]
        down = pltpu.roll(wrap * last, 1, 2)
        out = []
        for k in range(ks):
            at = rest + (k,)
            here = v[(n,) + at]
            if k < ks - 1:
                face = self.fy[(f,) + at]
                after = v[(n,) + rest + (k + 1,)]
                up = face * after
                next_down = face * here
            else:
                up = wrap * pltpu.roll(v[(n,) + rest + (0,)], 127, 2)
                next_down = None
            across = self.fx[(f,) + at] * v[(n - 1,) + at] + self.fx[(f + 1,) + at] * v[(n + 1,) + at]
            out.append((across + (up + down)) + z_pull(self.fz[(f,) + at], here))
            down = next_down
        return out

    def sweep(self, n, rest):
        moved = self.pull(self.g, n + 1, 0, rest)
        for k in range(self.ks):
            at = (n + 1,) + rest + (k,)
            self.e[(n,) + rest + (k,)] = BETA * self.g[at] + moved[k] * self.inv[at]

    def finish(self, n, rest):
        moved = self.pull(self.e, n + 1, 1, rest)
        out = []
        for k in range(self.ks):
            at = (n + 2,) + rest + (k,)
            out.append(
                (R1 * self.g[at] + R2 * self.e[(n + 1,) + rest + (k,)]) + moved[k] * self.inv[at]
            )
        return out


def kernel(
    node_f,
    node_c,
    w_f,
    w_c,
    mode_x,
    mode_y,
    mode_z,
    src_f,
    src_c,
    spread,
    gather,
    out,
    fraw,
    craw,
    nodes_f,
    nodes_c,
    weight_f,
    weight_c,
    mx,
    my_in,
    mz,
    mpad,
    xt,
    zt,
    spread_v,
    gather_v,
    mine,
    known,
    packed,
    fgot,
    fcs,
    rhs_f,
    rhs_c,
    c_f,
    fx_f,
    fy_f,
    fz_f,
    inv_f,
    g_f,
    e_f,
    c_c,
    fx_c,
    fy_c,
    fz_c,
    inv_c,
    g_c,
    e_c,
    wlane,
    qbuf,
    local_sem,
    node_send,
    node_recv,
    main_sem,
    extra_sem,
    rim_send,
    rim_recv,
):
    me_m = lax.axis_index("member")
    me_t = lax.axis_index("tile")
    parity = lax.rem(me_m, 2)
    half = me_m // 2

    def to(member, tile):
        return {"member": member, "tile": tile}

    def bring(index, source, target):
        copy = pltpu.make_async_copy(source, target, local_sem.at[index])
        copy.start()
        return copy

    own_nodes = [
        bring(0, node_f, nodes_f),
        bring(1, node_c, nodes_c),
        bring(2, w_f, weight_f),
        bring(3, w_c, weight_c),
    ]
    own_f = bring(4, src_f, fraw)
    own_c = bring(5, src_c, craw.at[:, pl.ds(8, 32)])
    modes = [
        bring(6, mode_x, mx),
        bring(7, mode_y, my_in),
        bring(8, mode_z, mz),
        bring(9, spread, spread_v),
        bring(10, gather, gather_v),
    ]

    barrier = pltpu.get_barrier_semaphore()

    def tell(device):
        pl.semaphore_signal(barrier, inc=1, device_id=device, device_id_type=MESH)

    for step in range(1, MEMBERS):
        tell(to(lax.rem(me_m + step, MEMBERS), me_t))
    aim = 4 * (half // 4) + lax.rem(half + me_t, 4)

    def aiming(strip):
        return to(2 * (4 * (me_t // 4) + lax.rem(me_t - strip + 2 * TILES, 4)) + parity, strip)

    owns = (half == me_t) & (aim == me_t)
    extra_source = half - 1 + 2 * parity
    extra_target = me_t + 1 - 2 * parity
    has_source = (extra_source >= 0) & (extra_source < TILES)
    at_home = (extra_target == half) & (aim == me_t)
    has_target = (extra_target >= 0) & (extra_target < TILES) & jnp.logical_not(at_home)
    waits_extra = has_source & jnp.logical_not(at_home)
    has_left = me_t > 0
    has_right = me_t < TILES - 1

    @pl.when(jnp.logical_not(owns))
    def _():
        tell(aiming(half))

    @pl.when(waits_extra)
    def _():
        tell(aiming(extra_source))

    @pl.when(has_left)
    def _():
        tell(to(me_m, me_t - 1))

    @pl.when(has_right)
    def _():
        tell(to(me_m, me_t + 1))

    lanes = iota((8, 128), 1)
    subs = iota((8, 128), 0)
    group = lanes & 7
    masks = (group == 0, group == 7, subs == 0, subs == 7)
    low_edge = (group == 0) & (me_t == 0)
    high_edge = (group == 7) & (me_t == TILES - 1)

    for copy in own_nodes:
        copy.wait()
    mine[...] = jnp.zeros((8, 128), F32)
    mine[0:1, 0:KL] = node_values(nodes_f[...])
    mine[1:5, 0:KL] = node_values(nodes_c[...])
    row = iota((8, 128), 0)
    weights = jnp.where(row == 0, jnp.broadcast_to(weight_f[...].astype(F32), (8, 128)), 0.0)
    for r in range(4):
        own_weight = jnp.broadcast_to(weight_c[:, r : r + 1].astype(F32), (8, 128))
        weights = jnp.where(row == r + 1, own_weight, weights)
    mine[...] = jnp.where(lanes == 15, weights, mine[...])

    def count(flag):
        return flag.astype(jnp.int32)

    pl.semaphore_wait(
        barrier,
        MEMBERS
        - count(owns)
        + count(has_target)
        + count(has_left)
        + count(has_right),
    )

    def node_copy(step):
        return pltpu.make_async_remote_copy(
            src_ref=mine,
            dst_ref=known.at[me_m],
            send_sem=node_send,
            recv_sem=node_recv,
            device_id=to(lax.rem(me_m + step, MEMBERS), me_t),
            device_id_type=MESH,
        )

    for step in range(1, MEMBERS):
        node_copy(step).start()
    known[me_m] = mine[...]

    def rim_copy(rightwards):
        if rightwards:
            return pltpu.make_async_remote_copy(
                src_ref=src_c.at[:, pl.ds(24, 8)],
                dst_ref=craw.at[:, pl.ds(0, 8)],
                send_sem=rim_send.at[0],
                recv_sem=rim_recv.at[0],
                device_id=to(me_m, lax.rem(me_t + 1, TILES)),
                device_id_type=MESH,
            )
        return pltpu.make_async_remote_copy(
            src_ref=src_c.at[:, pl.ds(0, 8)],
            dst_ref=craw.at[:, pl.ds(40, 8)],
            send_sem=rim_send.at[1],
            recv_sem=rim_recv.at[1],
            device_id=to(me_m, lax.rem(me_t + TILES - 1, TILES)),
            device_id_type=MESH,
        )

    @pl.when(has_right)
    def _():
        rim_copy(True).start()

    @pl.when(has_left)
    def _():
        rim_copy(False).start()

    craw[:, 48:64, :] = jnp.zeros((16, 16, 64), F32)

    @pl.when(jnp.logical_not(has_left))
    def _():
        craw[:, 0:8, :] = jnp.zeros((16, 8, 64), F32)

    @pl.when(jnp.logical_not(has_right))
    def _():
        craw[:, 40:48, :] = jnp.zeros((16, 8, 64), F32)

    own_f.wait()
    y = iota((512, 128), 0)
    col = iota((512, 128), 1)
    wanted = 64 * aim - 4 + KF * (col & 7) + (col >> 3)
    window = jnp.where((y == wanted) & (col < 8 * KF), 2.0, 0.0).astype(BF16)

    def pack(first, planes, at):
        high, low = halves(fraw[pl.ds(first, planes)].reshape(32 * planes, 512))
        got = jnp.dot(high, window, preferred_element_type=F32)
        got = got + jnp.dot(low, window, preferred_element_type=F32)
        packed[at : at + planes] = got.reshape(planes, 32, 128)

    pack(6 * parity, 10, 0)
    pack(14 - 14 * parity, 2, 10)

    main = pltpu.make_async_remote_copy(
        src_ref=packed.at[pl.ds(0, 10)],
        dst_ref=fgot.at[pl.ds(2 - 2 * parity, 10)],
        send_sem=main_sem.at[0],
        recv_sem=main_sem.at[1],
        device_id=to(2 * me_t + parity, aim),
        device_id_type=MESH,
    )
    extra = pltpu.make_async_remote_copy(
        src_ref=packed.at[pl.ds(10, 2)],
        dst_ref=fgot.at[pl.ds(10 * parity, 2)],
        send_sem=extra_sem.at[0],
        recv_sem=extra_sem.at[1],
        device_id=to(lax.rem(2 * extra_target + parity + MEMBERS, MEMBERS), aim),
        device_id_type=MESH,
    )

    @pl.when(jnp.logical_not(owns))
    def _():
        main.start()

    @pl.when(owns)
    def _():
        fgot[pl.ds(2 - 2 * parity, 10)] = packed[0:10]

    @pl.when(has_target)
    def _():
        extra.start()

    @pl.when(at_home)
    def _():
        fgot[pl.ds(10 * parity, 2)] = packed[10:12]

    @pl.when(jnp.logical_not(has_source))
    def _():
        fgot[pl.ds(10 * parity, 2)] = jnp.zeros((2, 32, 128), F32)

    for copy in modes:
        copy.wait()
    mpad[...] = jnp.zeros(mpad.shape, F32)
    mpad[0:KL, :] = my_in[...]
    fine_y = 64 * me_t - 4 + KF * (col & 7) + (col >> 3)
    coarse_y = 32 * me_t - 4 + KC * (col & 7) + ((col >> 3) - KF)
    picks = jnp.where(
        col < 8 * KF,
        jnp.where(y == fine_y, 1.0, 0.0),
        jnp.where(((y >> 1) == coarse_y) & (col < 8 * (KF + KC)), 0.5, 0.0),
    ).astype(BF16)
    parts = jnp.concatenate(thirds(mpad[...]), 0)
    my = jnp.dot(parts, picks, preferred_element_type=F32)
    my = (my[0:KP] + my[KP : 2 * KP]) + my[2 * KP : 3 * KP]
    own_col = iota((KP, 128), 1)
    fine_col = 64 * me_t - 4 + KF * (own_col & 7) + (own_col >> 3)
    coarse_col = 32 * me_t - 4 + KC * (own_col & 7) + ((own_col >> 3) - KF)
    reached = jnp.where(own_col < 8 * KF, fine_col, 2 * coarse_col)
    leaves = (reached < 0) | (reached >= 64 * TILES)
    my = jnp.where((iota((KP, 128), 0) == KL) & leaves, OUTSIDE, my)
    parts = jnp.concatenate(thirds(my), 0)
    wide = (KF + KC) * 128
    my = jnp.dot(parts, spread_v[:, 0:wide], preferred_element_type=F32)
    my = (my[0:KP] + my[KP : 2 * KP]) + my[2 * KP : 3 * KP]

    mpad[0:KL, 0:128] = mx[...]
    stacked = jnp.concatenate([mpad[:, 0:128]] * 8, 0)
    one = iota((XPAD, 128), 1)
    beyond = jnp.where((one == KL) | (one == KL + 1), 1.0, 0.0)
    xt[0:XPAD, :] = beyond
    xt[XPAD : XPAD + 128, :] = jnp.where(iota((128, 128), 1) == KL, 1.0, stacked.T)
    xt[XPAD + 128 : XPAD + 128 + XPAD, :] = beyond
    mpad[0:KL, 0:32] = mz[...]
    stacked = jnp.concatenate([mpad[:, 0:32]] * 8, 0)
    one = iota((32, 128), 1)
    zt[...] = jnp.where((one == KL) | (one == KL + 1), 1.0, stacked.T)
    zf = [zt[pl.ds(j, 8, stride=4), :] for j in range(4)]
    zc = [0.5 * (zf[2 * j] + zf[2 * j + 1]) for j in range(2)]
    zf = jnp.concatenate(zf, 0)
    zc = jnp.concatenate(zc, 0)

    def left(value):
        high = value.astype(BF16).astype(F32)
        return jnp.where(iota(value.shape, 1) < 32, high, value - high).astype(BF16)

    x0 = XF * me_m
    lhs_f = jnp.concatenate(
        [left(xt[pl.ds(x0 - 3 + XPAD + i, 1), :] * zf) for i in range(XF + 6)], 0
    )
    rows = []
    for i in range(XC + 6):
        at = x0 - 6 + XPAD + 2 * i
        mean = 0.5 * (xt[pl.ds(at, 1), :] + xt[pl.ds(at + 1, 1), :])
        rows.append(left(mean * zc))
    lhs_c = jnp.concatenate(rows, 0)
    rhs_f[64:128, :] = jnp.zeros((64, KF * 128), BF16)
    rhs_c[64:128, :] = jnp.zeros((64, KC * 512), BF16)

    arrivals = pltpu.make_async_remote_copy(
        src_ref=known.at[pl.ds(0, MEMBERS - 1)],
        dst_ref=known.at[pl.ds(0, MEMBERS - 1)],
        send_sem=node_send,
        recv_sem=node_recv,
        device_id=to(lax.rem(me_m + 1, MEMBERS), me_t),
        device_id_type=MESH,
    )
    arrivals.wait_recv()
    turned = known[...].reshape(128, 128).T[0:KP]
    parts = jnp.concatenate(thirds(turned), 0)
    pick = spread_v[:, wide : wide + 640]
    values = jnp.dot(parts, pick, preferred_element_type=F32)
    values = (values[0:KP] + values[KP : 2 * KP]) + values[2 * KP : 3 * KP]
    for r in range(5):
        scale = 0.125 * A3 if r == 0 else A3
        wlane[r] = jnp.broadcast_to(values[15:16, 128 * r : 128 * r + 128] * scale, (8, 128))

    def sides(value, factor):
        row = iota(value.shape, 0)
        scaled = jnp.where(row == KL, value, value * factor)
        high, low = halves(jnp.where(row == KL + 1, OUTSIDE, scaled))
        return jnp.concatenate([high, low, high, low], 0)

    for k in range(KF):
        at = slice(128 * k, 128 * k + 128)
        rhs_f[0:64, at] = sides(my[:, at], values[:, 0:128])
    for r in range(4):
        for k in range(KC):
            rhs_c[0:64, 128 * (KC * r + k) : 128 * (KC * r + k) + 128] = sides(
                my[:, 128 * (KF + k) : 128 * (KF + k) + 128],
                values[:, 128 * (r + 1) : 128 * (r + 1) + 128],
            )

    logs = jnp.dot(lhs_f, rhs_f[...], preferred_element_type=F32)
    for i in range(XF + 6):
        for k in range(KF):
            c_f[i, k] = jnp.exp2(
                logs[32 * i : 32 * i + 32, 128 * k : 128 * k + 128]
            ).reshape(4, 8, 128)
    logs = jnp.dot(lhs_c, rhs_c[...], preferred_element_type=F32)
    for i in range(XC + 6):
        for r in range(4):
            for k in range(KC):
                at = 128 * (KC * r + k)
                c_c[i, r, k] = jnp.exp2(logs[16 * i : 16 * i + 16, at : at + 128]).reshape(2, 8, 128)

    fine = Level(KF, c_f, fx_f, fy_f, fz_f, inv_f, g_f, e_f)
    coarse = Level(KC, c_c, fx_c, fy_c, fz_c, inv_c, g_c, e_c)

    def hide_fine(k):
        return ([low_edge] if k < 4 else []) + ([high_edge] if k >= 5 else [])

    def hide_coarse(k):
        return ([low_edge] if k < 4 else []) + ([high_edge] if k >= 1 else [])

    def clear(inv, planes):
        @pl.when(me_m == 0)
        def _():
            inv[0:2] = jnp.zeros((2,) + inv.shape[1:], F32)

        @pl.when(me_m == MEMBERS - 1)
        def _():
            inv[planes - 2 : planes] = jnp.zeros((2,) + inv.shape[1:], F32)

    fx_f[0] = c_f[0] + c_f[1]
    fx_c[0] = c_c[0] + c_c[1]

    def set_fine(n, carry):
        fine.set_up(n, (), masks, hide_fine)
        return carry

    lax.fori_loop(0, XF + 4, set_fine, 0)
    clear(inv_f, XF + 4)

    def set_coarse(n, carry):
        for r in range(4):
            coarse.set_up(n, (r,), masks, hide_coarse)
        return carry

    lax.fori_loop(0, XC + 4, set_coarse, 0)
    clear(inv_c, XC + 4)

    @pl.when(jnp.logical_not(owns))
    def _():
        main.wait_recv()

    @pl.when(waits_extra)
    def _():
        extra.wait_recv()

    for chunk in range(3):
        rows = []
        for i in range(4):
            for j in range(4):
                rows.append(fgot[4 * chunk + i, pl.ds(j, 8, stride=4), :])
        high, low = halves(jnp.concatenate(rows, 0))
        got = jnp.dot(high, spread_v[:, 0 : KF * 128], preferred_element_type=F32)
        got = got + jnp.dot(low, spread_v[:, 0 : KF * 128], preferred_element_type=F32)
        for i in range(4):
            n = 4 * chunk + i
            for k in range(KF):
                g_f[n, k] = (
                    got[32 * i : 32 * i + 32, 128 * k : 128 * k + 128].reshape(4, 8, 128) * inv_f[n, k]
                )

    own_c.wait()

    @pl.when(has_left)
    def _():
        rim_copy(True).wait_recv()

    @pl.when(has_right)
    def _():
        rim_copy(False).wait_recv()

    chosen = (iota((16, 64), 1) == 4 * me_m - 2 + iota((16, 64), 0)) & (iota((16, 64), 0) < 8)
    chosen = jnp.where(chosen, 1.0, 0.0).astype(BF16)
    contract = (((1,), (1,)), ((), ()))
    planes = 0.0
    for part in halves(craw[...].reshape(1024, 64)):
        planes = planes + lax.dot_general(chosen, part, contract, preferred_element_type=F32)
    rows = jnp.concatenate([planes[0:8, 128 * p : 128 * p + 128] for p in range(8)], 0)
    high, low = halves(rows)
    order = spread_v[:, wide + 640 : wide + 640 + KC * 256]
    got = jnp.dot(high, order, preferred_element_type=F32)
    got = got + jnp.dot(low, order, preferred_element_type=F32)
    for p in range(8):
        for j in range(2):
            for k in range(KC):
                at = 128 * (KC * j + k)
                fcs[pl.ds(16 * k + 8 * j + p, 8, stride=16 * KC), :] = got[
                    8 * p : 8 * p + 8, at : at + 128
                ]
    for n in range(XC + 4):
        for k in range(KC):
            at = 16 * (KC * n + k)
            source = fcs[at : at + 16, :].reshape(2, 8, 128)
            for r in range(4):
                g_c[n, r, k] = source * inv_c[n, r, k]

    def sweep_fine(n, carry):
        fine.sweep(n, ())
        return carry

    lax.fori_loop(0, XF + 2, sweep_fine, 0)

    def sweep_coarse(n, carry):
        for r in range(4):
            coarse.sweep(n, (r,))
        return carry

    lax.fori_loop(0, XC + 2, sweep_coarse, 0)

    def finish(xc, carry):
        base = pl.multiple_of(16 * xc, 16)
        low, high = fine.finish(2 * xc, ()), fine.finish(2 * xc + 1, ())
        for k in range(KF):
            pair = low[k] + high[k]
            for j in range(2):
                qbuf[pl.ds(base + 8 * j, 8), 128 * k : 128 * k + 128] = wlane[0] * (
                    pair[2 * j] + pair[2 * j + 1]
                )
        terms = [coarse.finish(xc, (r,)) for r in range(4)]
        for k in range(KC):
            at = 128 * (KF + k)
            both = (wlane[1] * terms[0][k] + wlane[2] * terms[1][k]) + (
                wlane[3] * terms[2][k] + wlane[4] * terms[3][k]
            )
            qbuf[pl.ds(base, 16), at : at + 128] = both.reshape(16, 128)
        return carry

    lax.fori_loop(0, XC, finish, 0)

    high, low = halves(qbuf[...])
    total = jnp.dot(high, gather_v[...], preferred_element_type=F32)
    total = total + jnp.dot(low, gather_v[...], preferred_element_type=F32)
    for xc in range(XC):
        for j in range(2):
            at = 16 * xc + 8 * j
            out[xc, pl.ds(j, 8, stride=2), :] = total[at : at + 8, 0:32]

    arrivals.wait_send()

    @pl.when(has_right)
    def _():
        rim_copy(True).wait_send()

    @pl.when(has_left)
    def _():
        rim_copy(False).wait_send()

    @pl.when(jnp.logical_not(owns))
    def _():
        main.wait_send()

    @pl.when(has_target)
    def _():
        extra.wait_send()


def matrices():
    lane = np.arange(128)
    group = lane % 8
    spread = np.zeros((128, 128 * (KF + KC) + 640 + 256 * KC), np.float32)
    for k in range(KF + KC):
        spread[8 * k + group, 128 * k + lane] = 1.0
    base = 128 * (KF + KC)
    for r in range(5):
        spread[8 * (lane // 8) + r, base + 128 * r + lane] = 1.0
    base += 640
    for j in range(2):
        for k in range(KC):
            spread[64 * j + 4 + KC * group + k, base + 128 * (KC * j + k) + lane] = 2.0
    gather = np.zeros((128 * (KF + KC), 32), np.float32)
    for k in range(KF + KC):
        target = (KF * group + k - 4) // 2 if k < KF else KC * group + (k - KF) - 4
        ok = (target >= 0) & (target < 32)
        gather[128 * k + lane[ok], target[ok]] = 1.0
    return jnp.asarray(spread, BF16), jnp.asarray(gather, BF16)


def body(
    node_fine,
    node_coarse,
    weight_fine,
    weight_coarse,
    mode_x,
    mode_y,
    mode_z,
    source_fine,
    source_coarse,
):
    hbm = pl.BlockSpec(memory_space=pl.ANY)
    fine = (KF, 4, 8, 128)
    coarse = (4, KC, 2, 8, 128)
    dma = pltpu.SemaphoreType.DMA

    def vmem(*shape, dtype=F32):
        return pltpu.VMEM(shape, dtype)

    wide = 128 * (KF + KC)
    scratch = [
        vmem(16, 32, 512),
        vmem(16, 64, 64),
        vmem(1, KL, dtype=jnp.int32),
        vmem(4, KL, dtype=jnp.int32),
        vmem(1, 1, dtype=jnp.int32),
        vmem(1, 4, dtype=jnp.int32),
        vmem(KL, 128),
        vmem(KL, 512),
        vmem(KL, 32),
        vmem(KP, 512),
        vmem(XPAD + 128 + XPAD, 128),
        vmem(32, 128),
        vmem(128, wide + 640 + 256 * KC, dtype=BF16),
        vmem(wide, 32, dtype=BF16),
        vmem(8, 128),
        vmem(MEMBERS, 8, 128),
        vmem(12, 32, 128),
        vmem(12, 32, 128),
        vmem(128 * KC, 128),
        vmem(128, KF * 128, dtype=BF16),
        vmem(128, KC * 512, dtype=BF16),
        vmem(XF + 6, *fine),
        vmem(XF + 5, *fine),
        vmem(XF + 4, *fine),
        vmem(XF + 4, *fine),
        vmem(XF + 4, *fine),
        vmem(XF + 4, *fine),
        vmem(XF + 2, *fine),
        vmem(XC + 6, *coarse),
        vmem(XC + 5, *coarse),
        vmem(XC + 4, *coarse),
        vmem(XC + 4, *coarse),
        vmem(XC + 4, *coarse),
        vmem(XC + 4, *coarse),
        vmem(XC + 2, *coarse),
        vmem(5, 8, 128),
        vmem(64, wide),
        dma((11,)),
        dma(()),
        dma(()),
        dma((2,)),
        dma((2,)),
        dma((2,)),
        dma((2,)),
    ]
    return pl.pallas_call(
        kernel,
        out_shape=jax.ShapeDtypeStruct((4, 16, 32), F32),
        in_specs=[hbm] * 11,
        out_specs=pl.BlockSpec(memory_space=pltpu.VMEM),
        scratch_shapes=scratch,
        compiler_params=pltpu.CompilerParams(
            collective_id=0, has_side_effects=True, vmem_limit_bytes=60 * 2**20
        ),
    )(
        node_fine,
        node_coarse,
        weight_fine.reshape(1, 1),
        weight_coarse.reshape(1, 4),
        mode_x,
        mode_y,
        mode_z,
        source_fine,
        jnp.transpose(source_coarse, (1, 2, 0)),
        *matrices(),
    )


def solution(mesh):
    return jax.shard_map(
        body,
        mesh=mesh,
        in_specs=(
            P("member", None),
            P("member", None),
            P("member"),
            P("member"),
            P(),
            P(),
            P(),
            P("tile", None, None),
            P(None, None, "tile"),
        ),
        out_specs=P("member", None, "tile"),
        check_vma=False,
    )
```

```python
import math

import jax
import jax.numpy as jnp
import numpy as np
from jax import lax
from jax.experimental import pallas as pl
from jax.experimental.pallas import tpu as pltpu
from jax.sharding import PartitionSpec as P

NODES = 9
SWEEPS = 3
CENTRE = 1.125
HALF_WIDTH = 0.875
SPREAD_RATIO = CENTRE / HALF_WIDTH
LOG2E = 1.0 / math.log(2.0)

F32 = jnp.float32
BF16 = jnp.bfloat16
MESH = pl.DeviceIdType.MESH

TILES = 8
MEMBERS = 16
KL = 12
KP = 16
XF = 8
XC = 4
KF = 9
KC = 5
XPAD = 8
OUTSIDE = -1024.0


def sweep_factors(sweep_count):
    previous = 1.0 / SPREAD_RATIO
    factors = []
    for _ in range(sweep_count - 1):
        current = 1.0 / (2.0 * SPREAD_RATIO - previous)
        factors.append((current * previous, 2.0 * current / HALF_WIDTH))
        previous = current
    return factors


(KEEP1, PUSH1), (KEEP2, PUSH2) = sweep_factors(SWEEPS)
FIRST = 1.0 / CENTRE
SHARE = (1.0 - FIRST) / FIRST
SECOND = PUSH1 * FIRST
BETA = KEEP1 / PUSH1 + SHARE
LEFT = (1.0 - PUSH1) * FIRST
A1 = FIRST + PUSH2 * (LEFT * (SHARE - BETA) - KEEP1 * FIRST)
A2 = (1.0 + KEEP2) * SECOND + PUSH2 * LEFT
A3 = PUSH2 * SECOND
R1 = A1 / A3
R2 = A2 / A3


def iota(shape, dim):
    return lax.broadcasted_iota(jnp.int32, shape, dim)


def halves(value):
    high = value.astype(BF16)
    return high, (value - high.astype(F32)).astype(BF16)


def thirds(value):
    high = value.astype(BF16)
    rest = value - high.astype(F32)
    middle = rest.astype(BF16)
    return high, middle, (rest - middle.astype(F32)).astype(BF16)


def cut(value, low, high, axis):
    return lax.slice_in_dim(value, low, high, axis=axis)


def node_values(index):
    value = jnp.zeros(index.shape, F32)
    for node in range(NODES):
        value = jnp.where(index == node, math.cos(math.pi * node / (NODES - 1)) * LOG2E, value)
    return value


def z_faces(c, masks):
    n = c.shape[0]
    wrap = c[n - 1 : n] + jnp.where(masks[3], 0.0, pltpu.roll(c[0:1], 7, 1))
    closed = jnp.where(masks[3], 0.0, wrap)
    inner = c[0 : n - 1] + c[1:n]
    down = jnp.where(masks[2], c[0:1], pltpu.roll(closed, 1, 1))
    up = jnp.concatenate([inner, wrap], 0)
    return jnp.concatenate([inner, closed], 0), up + jnp.concatenate([down, inner], 0)


def z_pull(face, v):
    n = v.shape[0]
    inner, wrap = face[0 : n - 1], face[n - 1 : n]
    up = jnp.concatenate([inner * v[1:n], wrap * pltpu.roll(v[0:1], 7, 1)], 0)
    down = jnp.concatenate([pltpu.roll(wrap * v[n - 1 : n], 1, 1), inner * v[0 : n - 1]], 0)
    return up + down


class Level:
    def __init__(self, ks, c, fx, fy, fz, inv, g, e):
        self.ks, self.c, self.fx, self.fy, self.fz = ks, c, fx, fy, fz
        self.inv, self.g, self.e = inv, g, e

    def set_up(self, n, rest, masks, hide):
        ks = self.ks
        c = [self.c[(n + 1,) + rest + (k,)] for k in range(ks)]
        wrap = c[ks - 1] + jnp.where(masks[1], 0.0, pltpu.roll(c[0], 127, 2))
        closed = jnp.where(masks[1], 0.0, wrap)
        down = jnp.where(masks[0], c[0], pltpu.roll(closed, 1, 2))
        for k in range(ks):
            upper = c[k] + self.c[(n + 2,) + rest + (k,)]
            next_face = c[k] + c[k + 1] if k < ks - 1 else wrap
            z_face, z_sum = z_faces(c[k], masks)
            total = ((self.fx[(n,) + rest + (k,)] + upper) + (next_face + down)) + z_sum
            turned = pltpu.reciprocal(total, approx=True)
            for mask in hide(k):
                turned = jnp.where(mask, 0.0, turned)
            self.fx[(n + 1,) + rest + (k,)] = upper
            self.fy[(n,) + rest + (k,)] = next_face if k < ks - 1 else closed
            self.fz[(n,) + rest + (k,)] = z_face
            self.inv[(n,) + rest + (k,)] = turned
            down = next_face

    def pull(self, v, n, shift, rest):
        ks = self.ks
        f = n + shift
        last = v[(n,) + rest + (ks - 1,)]
        wrap = self.fy[(f,) + rest + (ks - 1,)]
        down = pltpu.roll(wrap * last, 1, 2)
        out = []
        for k in range(ks):
            at = rest + (k,)
            here = v[(n,) + at]
            if k < ks - 1:
                face = self.fy[(f,) + at]
                after = v[(n,) + rest + (k + 1,)]
                up = face * after
                next_down = face * here
            else:
                up = wrap * pltpu.roll(v[(n,) + rest + (0,)], 127, 2)
                next_down = None
            across = self.fx[(f,) + at] * v[(n - 1,) + at] + self.fx[(f + 1,) + at] * v[(n + 1,) + at]
            out.append((across + (up + down)) + z_pull(self.fz[(f,) + at], here))
            down = next_down
        return out

    def sweep(self, n, rest):
        moved = self.pull(self.g, n + 1, 0, rest)
        for k in range(self.ks):
            at = (n + 1,) + rest + (k,)
            self.e[(n,) + rest + (k,)] = BETA * self.g[at] + moved[k] * self.inv[at]

    def finish(self, n, rest):
        moved = self.pull(self.e, n + 1, 1, rest)
        out = []
        for k in range(self.ks):
            at = (n + 2,) + rest + (k,)
            out.append(
                (R1 * self.g[at] + R2 * self.e[(n + 1,) + rest + (k,)]) + moved[k] * self.inv[at]
            )
        return out


def kernel(
    node_f,
    node_c,
    w_f,
    w_c,
    mode_x,
    mode_y,
    mode_z,
    src_f,
    src_c,
    spread,
    gather,
    out,
    fraw,
    craw,
    nodes_f,
    nodes_c,
    weight_f,
    weight_c,
    mx,
    my_in,
    mz,
    mpad,
    xt,
    zt,
    spread_v,
    gather_v,
    mine,
    known,
    packed,
    fgot,
    fcs,
    rhs_f,
    rhs_c,
    double_f,
    double_c,
    c_f,
    fx_f,
    fy_f,
    fz_f,
    inv_f,
    g_f,
    e_f,
    c_c,
    fx_c,
    fy_c,
    fz_c,
    inv_c,
    g_c,
    e_c,
    wlane,
    qbuf,
    local_sem,
    node_send,
    node_recv,
    main_sem,
    extra_sem,
    rim_send,
    rim_recv,
):
    me_m = lax.axis_index("member")
    me_t = lax.axis_index("tile")
    parity = lax.rem(me_m, 2)
    half = me_m // 2

    def to(member, tile):
        return {"member": member, "tile": tile}

    def bring(index, source, target):
        copy = pltpu.make_async_copy(source, target, local_sem.at[index])
        copy.start()
        return copy

    own_nodes = [
        bring(0, node_f, nodes_f),
        bring(1, node_c, nodes_c),
        bring(2, w_f, weight_f),
        bring(3, w_c, weight_c),
    ]
    own_f = bring(4, src_f, fraw)
    own_c = bring(5, src_c, craw.at[:, pl.ds(8, 32)])
    modes = [
        bring(6, mode_x, mx),
        bring(7, mode_y, my_in),
        bring(8, mode_z, mz),
        bring(9, spread, spread_v),
        bring(10, gather, gather_v),
    ]

    barrier = pltpu.get_barrier_semaphore()

    def tell(device):
        pl.semaphore_signal(barrier, inc=1, device_id=device, device_id_type=MESH)

    for step in range(1, MEMBERS):
        tell(to(lax.rem(me_m + step, MEMBERS), me_t))
    aim = 4 * (half // 4) + lax.rem(half + me_t, 4)

    def aiming(strip):
        return to(2 * (4 * (me_t // 4) + lax.rem(me_t - strip + 2 * TILES, 4)) + parity, strip)

    owns = (half == me_t) & (aim == me_t)
    extra_source = half - 1 + 2 * parity
    extra_target = me_t + 1 - 2 * parity
    has_source = (extra_source >= 0) & (extra_source < TILES)
    at_home = (extra_target == half) & (aim == me_t)
    has_target = (extra_target >= 0) & (extra_target < TILES) & jnp.logical_not(at_home)
    waits_extra = has_source & jnp.logical_not(at_home)
    has_left = me_t > 0
    has_right = me_t < TILES - 1

    @pl.when(jnp.logical_not(owns))
    def _():
        tell(aiming(half))

    @pl.when(waits_extra)
    def _():
        tell(aiming(extra_source))

    @pl.when(has_left)
    def _():
        tell(to(me_m, me_t - 1))

    @pl.when(has_right)
    def _():
        tell(to(me_m, me_t + 1))

    lanes = iota((8, 128), 1)
    subs = iota((8, 128), 0)
    group = lanes & 7
    masks = (group == 0, group == 7, subs == 0, subs == 7)
    low_edge = (group == 0) & (me_t == 0)
    high_edge = (group == 7) & (me_t == TILES - 1)

    for copy in own_nodes:
        copy.wait()
    mine[...] = jnp.zeros((8, 128), F32)
    mine[0:1, 0:KL] = node_values(nodes_f[...])
    mine[1:5, 0:KL] = node_values(nodes_c[...])
    row = iota((8, 128), 0)
    weights = jnp.where(row == 0, jnp.broadcast_to(weight_f[...].astype(F32), (8, 128)), 0.0)
    for r in range(4):
        own_weight = jnp.broadcast_to(weight_c[:, r : r + 1].astype(F32), (8, 128))
        weights = jnp.where(row == r + 1, own_weight, weights)
    mine[...] = jnp.where(lanes == 15, weights, mine[...])

    def count(flag):
        return flag.astype(jnp.int32)

    pl.semaphore_wait(
        barrier,
        MEMBERS
        - count(owns)
        + count(has_target)
        + count(has_left)
        + count(has_right),
    )

    def node_copy(step):
        return pltpu.make_async_remote_copy(
            src_ref=mine,
            dst_ref=known.at[me_m],
            send_sem=node_send,
            recv_sem=node_recv,
            device_id=to(lax.rem(me_m + step, MEMBERS), me_t),
            device_id_type=MESH,
        )

    for step in range(1, MEMBERS):
        node_copy(step).start()
    known[me_m] = mine[...]

    def rim_copy(rightwards):
        if rightwards:
            return pltpu.make_async_remote_copy(
                src_ref=src_c.at[:, pl.ds(24, 8)],
                dst_ref=craw.at[:, pl.ds(0, 8)],
                send_sem=rim_send.at[0],
                recv_sem=rim_recv.at[0],
                device_id=to(me_m, lax.rem(me_t + 1, TILES)),
                device_id_type=MESH,
            )
        return pltpu.make_async_remote_copy(
            src_ref=src_c.at[:, pl.ds(0, 8)],
            dst_ref=craw.at[:, pl.ds(40, 8)],
            send_sem=rim_send.at[1],
            recv_sem=rim_recv.at[1],
            device_id=to(me_m, lax.rem(me_t + TILES - 1, TILES)),
            device_id_type=MESH,
        )

    @pl.when(has_right)
    def _():
        rim_copy(True).start()

    @pl.when(has_left)
    def _():
        rim_copy(False).start()

    craw[:, 48:64, :] = jnp.zeros((16, 16, 64), F32)

    @pl.when(jnp.logical_not(has_left))
    def _():
        craw[:, 0:8, :] = jnp.zeros((16, 8, 64), F32)

    @pl.when(jnp.logical_not(has_right))
    def _():
        craw[:, 40:48, :] = jnp.zeros((16, 8, 64), F32)

    own_f.wait()
    y = iota((512, 128), 0)
    col = iota((512, 128), 1)
    wanted = 64 * aim - 4 + KF * (col & 7) + (col >> 3)
    window = jnp.where((y == wanted) & (col < 8 * KF), 2.0, 0.0).astype(BF16)

    def pack(first, planes, at):
        high, low = halves(fraw[pl.ds(first, planes)].reshape(32 * planes, 512))
        got = jnp.dot(high, window, preferred_element_type=F32)
        got = got + jnp.dot(low, window, preferred_element_type=F32)
        packed[at : at + planes] = got.reshape(planes, 32, 128)

    pack(6 * parity, 10, 0)
    pack(14 - 14 * parity, 2, 10)

    main = pltpu.make_async_remote_copy(
        src_ref=packed.at[pl.ds(0, 10)],
        dst_ref=fgot.at[pl.ds(2 - 2 * parity, 10)],
        send_sem=main_sem.at[0],
        recv_sem=main_sem.at[1],
        device_id=to(2 * me_t + parity, aim),
        device_id_type=MESH,
    )
    extra = pltpu.make_async_remote_copy(
        src_ref=packed.at[pl.ds(10, 2)],
        dst_ref=fgot.at[pl.ds(10 * parity, 2)],
        send_sem=extra_sem.at[0],
        recv_sem=extra_sem.at[1],
        device_id=to(lax.rem(2 * extra_target + parity + MEMBERS, MEMBERS), aim),
        device_id_type=MESH,
    )

    @pl.when(jnp.logical_not(owns))
    def _():
        main.start()

    @pl.when(owns)
    def _():
        fgot[pl.ds(2 - 2 * parity, 10)] = packed[0:10]

    @pl.when(has_target)
    def _():
        extra.start()

    @pl.when(at_home)
    def _():
        fgot[pl.ds(10 * parity, 2)] = packed[10:12]

    @pl.when(jnp.logical_not(has_source))
    def _():
        fgot[pl.ds(10 * parity, 2)] = jnp.zeros((2, 32, 128), F32)

    for copy in modes:
        copy.wait()
    mpad[...] = jnp.zeros(mpad.shape, F32)
    mpad[0:KL, :] = my_in[...]
    fine_y = 64 * me_t - 4 + KF * (col & 7) + (col >> 3)
    coarse_y = 32 * me_t - 4 + KC * (col & 7) + ((col >> 3) - KF)
    picks = jnp.where(
        col < 8 * KF,
        jnp.where(y == fine_y, 1.0, 0.0),
        jnp.where(((y >> 1) == coarse_y) & (col < 8 * (KF + KC)), 0.5, 0.0),
    ).astype(BF16)
    parts = jnp.concatenate(thirds(mpad[...]), 0)
    my = jnp.dot(parts, picks, preferred_element_type=F32)
    my = (my[0:KP] + my[KP : 2 * KP]) + my[2 * KP : 3 * KP]
    own_col = iota((KP, 128), 1)
    fine_col = 64 * me_t - 4 + KF * (own_col & 7) + (own_col >> 3)
    coarse_col = 32 * me_t - 4 + KC * (own_col & 7) + ((own_col >> 3) - KF)
    reached = jnp.where(own_col < 8 * KF, fine_col, 2 * coarse_col)
    leaves = (reached < 0) | (reached >= 64 * TILES)
    my = jnp.where((iota((KP, 128), 0) == KL) & leaves, OUTSIDE, my)
    parts = jnp.concatenate(thirds(my), 0)
    wide = (KF + KC) * 128
    my = jnp.dot(parts, spread_v[:, 0:wide], preferred_element_type=F32)
    my = (my[0:KP] + my[KP : 2 * KP]) + my[2 * KP : 3 * KP]

    mpad[0:KL, 0:128] = mx[...]
    stacked = jnp.concatenate([mpad[:, 0:128]] * 8, 0)
    one = iota((XPAD, 128), 1)
    beyond = jnp.where((one == KL) | (one == KL + 1), 1.0, 0.0)
    xt[0:XPAD, :] = beyond
    xt[XPAD : XPAD + 128, :] = jnp.where(iota((128, 128), 1) == KL, 1.0, stacked.T)
    xt[XPAD + 128 : XPAD + 128 + XPAD, :] = beyond
    mpad[0:KL, 0:32] = mz[...]
    stacked = jnp.concatenate([mpad[:, 0:32]] * 8, 0)
    one = iota((32, 128), 1)
    zt[...] = jnp.where((one == KL) | (one == KL + 1), 1.0, stacked.T)
    zf = [zt[pl.ds(j, 8, stride=4), :] for j in range(4)]
    zc = [0.5 * (zf[2 * j] + zf[2 * j + 1]) for j in range(2)]
    zf = jnp.concatenate(zf, 0)
    zc = jnp.concatenate(zc, 0)

    def left(value):
        high = value.astype(BF16).astype(F32)
        return jnp.where(iota(value.shape, 1) < 32, high, value - high).astype(BF16)

    x0 = XF * me_m
    lhs_f = jnp.concatenate(
        [left(xt[pl.ds(x0 - 3 + XPAD + i, 1), :] * zf) for i in range(XF + 6)], 0
    )
    rows = []
    for i in range(XC + 6):
        at = x0 - 6 + XPAD + 2 * i
        mean = 0.5 * (xt[pl.ds(at, 1), :] + xt[pl.ds(at + 1, 1), :])
        rows.append(left(mean * zc))
    lhs_c = jnp.concatenate(rows, 0)
    rhs_f[64:128, :] = jnp.zeros((64, KF * 128), BF16)
    rhs_c[64:128, :] = jnp.zeros((64, KC * 512), BF16)

    wide_end = wide + 640
    for part in range(2):
        double_f[128 * part : 128 * part + 128, :] = spread_v[:, 0 : KF * 128]
        double_c[128 * part : 128 * part + 128, :] = spread_v[:, wide_end : wide_end + KC * 256]

    arrivals = pltpu.make_async_remote_copy(
        src_ref=known.at[pl.ds(0, MEMBERS - 1)],
        dst_ref=known.at[pl.ds(0, MEMBERS - 1)],
        send_sem=node_send,
        recv_sem=node_recv,
        device_id=to(lax.rem(me_m + 1, MEMBERS), me_t),
        device_id_type=MESH,
    )
    arrivals.wait_recv()
    turned = known[...].reshape(128, 128).T[0:KP]
    parts = jnp.concatenate(thirds(turned), 0)
    pick = spread_v[:, wide : wide + 640]
    values = jnp.dot(parts, pick, preferred_element_type=F32)
    values = (values[0:KP] + values[KP : 2 * KP]) + values[2 * KP : 3 * KP]
    for r in range(5):
        scale = 0.125 * A3 if r == 0 else A3
        wlane[r] = jnp.broadcast_to(values[15:16, 128 * r : 128 * r + 128] * scale, (8, 128))

    def sides(value, factor):
        row = iota(value.shape, 0)
        scaled = jnp.where(row == KL, value, value * factor)
        high, low = halves(jnp.where(row == KL + 1, OUTSIDE, scaled))
        return jnp.concatenate([high, low, high, low], 0)

    for k in range(KF):
        at = slice(128 * k, 128 * k + 128)
        rhs_f[0:64, at] = sides(my[:, at], values[:, 0:128])
    for r in range(4):
        for k in range(KC):
            rhs_c[0:64, 128 * (KC * r + k) : 128 * (KC * r + k) + 128] = sides(
                my[:, 128 * (KF + k) : 128 * (KF + k) + 128],
                values[:, 128 * (r + 1) : 128 * (r + 1) + 128],
            )

    logs = jnp.dot(lhs_f, rhs_f[...], preferred_element_type=F32)
    for i in range(XF + 6):
        for k in range(KF):
            c_f[i, k] = jnp.exp2(
                logs[32 * i : 32 * i + 32, 128 * k : 128 * k + 128]
            ).reshape(4, 8, 128)
    logs = jnp.dot(lhs_c, rhs_c[...], preferred_element_type=F32)
    for i in range(XC + 6):
        for r in range(4):
            for k in range(KC):
                at = 128 * (KC * r + k)
                c_c[i, r, k] = jnp.exp2(logs[16 * i : 16 * i + 16, at : at + 128]).reshape(2, 8, 128)

    fine = Level(KF, c_f, fx_f, fy_f, fz_f, inv_f, g_f, e_f)
    coarse = Level(KC, c_c, fx_c, fy_c, fz_c, inv_c, g_c, e_c)

    def hide_fine(k):
        return ([low_edge] if k < 4 else []) + ([high_edge] if k >= 5 else [])

    def hide_coarse(k):
        return ([low_edge] if k < 4 else []) + ([high_edge] if k >= 1 else [])

    def clear(inv, planes):
        @pl.when(me_m == 0)
        def _():
            inv[0:2] = jnp.zeros((2,) + inv.shape[1:], F32)

        @pl.when(me_m == MEMBERS - 1)
        def _():
            inv[planes - 2 : planes] = jnp.zeros((2,) + inv.shape[1:], F32)

    fx_f[0] = c_f[0] + c_f[1]
    fx_c[0] = c_c[0] + c_c[1]

    def set_fine(n, carry):
        fine.set_up(n, (), masks, hide_fine)
        return carry

    lax.fori_loop(0, XF + 4, set_fine, 0, unroll=2)
    clear(inv_f, XF + 4)

    def set_coarse(n, carry):
        for r in range(4):
            coarse.set_up(n, (r,), masks, hide_coarse)
        return carry

    lax.fori_loop(0, XC + 4, set_coarse, 0, unroll=2)
    clear(inv_c, XC + 4)

    @pl.when(jnp.logical_not(owns))
    def _():
        main.wait_recv()

    @pl.when(waits_extra)
    def _():
        extra.wait_recv()

    for chunk in range(3):
        rows = []
        for i in range(4):
            for j in range(4):
                rows.append(fgot[4 * chunk + i, pl.ds(j, 8, stride=4), :])
        high, low = halves(jnp.concatenate(rows, 0))
        got = jnp.dot(
            jnp.concatenate([high, low], 1), double_f[...], preferred_element_type=F32
        )
        for i in range(4):
            n = 4 * chunk + i
            for k in range(KF):
                g_f[n, k] = (
                    got[32 * i : 32 * i + 32, 128 * k : 128 * k + 128].reshape(4, 8, 128) * inv_f[n, k]
                )

    own_c.wait()

    @pl.when(has_left)
    def _():
        rim_copy(True).wait_recv()

    @pl.when(has_right)
    def _():
        rim_copy(False).wait_recv()

    chosen = (iota((16, 64), 1) == 4 * me_m - 2 + iota((16, 64), 0)) & (iota((16, 64), 0) < 8)
    chosen = jnp.where(chosen, 1.0, 0.0).astype(BF16)
    contract = (((1,), (1,)), ((), ()))
    planes = 0.0
    for part in halves(craw[...].reshape(1024, 64)):
        planes = planes + lax.dot_general(chosen, part, contract, preferred_element_type=F32)
    rows = jnp.concatenate([planes[0:8, 128 * p : 128 * p + 128] for p in range(8)], 0)
    high, low = halves(rows)
    got = jnp.dot(jnp.concatenate([high, low], 1), double_c[...], preferred_element_type=F32)
    for p in range(8):
        for j in range(2):
            for k in range(KC):
                at = 128 * (KC * j + k)
                fcs[pl.ds(16 * k + 8 * j + p, 8, stride=16 * KC), :] = got[
                    8 * p : 8 * p + 8, at : at + 128
                ]
    for n in range(XC + 4):
        for k in range(KC):
            at = 16 * (KC * n + k)
            source = fcs[at : at + 16, :].reshape(2, 8, 128)
            for r in range(4):
                g_c[n, r, k] = source * inv_c[n, r, k]

    def sweep_fine(n, carry):
        fine.sweep(n, ())
        return carry

    lax.fori_loop(0, XF + 2, sweep_fine, 0, unroll=2)

    def sweep_coarse(n, carry):
        for r in range(4):
            coarse.sweep(n, (r,))
        return carry

    lax.fori_loop(0, XC + 2, sweep_coarse, 0, unroll=2)

    def finish(xc, carry):
        base = pl.multiple_of(16 * xc, 16)
        low, high = fine.finish(2 * xc, ()), fine.finish(2 * xc + 1, ())
        for k in range(KF):
            pair = low[k] + high[k]
            for j in range(2):
                qbuf[pl.ds(base + 8 * j, 8), 128 * k : 128 * k + 128] = wlane[0] * (
                    pair[2 * j] + pair[2 * j + 1]
                )
        terms = [coarse.finish(xc, (r,)) for r in range(4)]
        for k in range(KC):
            at = 128 * (KF + k)
            both = (wlane[1] * terms[0][k] + wlane[2] * terms[1][k]) + (
                wlane[3] * terms[2][k] + wlane[4] * terms[3][k]
            )
            qbuf[pl.ds(base, 16), at : at + 128] = both.reshape(16, 128)
        return carry

    lax.fori_loop(0, XC, finish, 0)

    high, low = halves(qbuf[...])
    total = jnp.dot(high, gather_v[...], preferred_element_type=F32)
    total = total + jnp.dot(low, gather_v[...], preferred_element_type=F32)
    for xc in range(XC):
        for j in range(2):
            at = 16 * xc + 8 * j
            out[xc, pl.ds(j, 8, stride=2), :] = total[at : at + 8, 0:32]

    arrivals.wait_send()

    @pl.when(has_right)
    def _():
        rim_copy(True).wait_send()

    @pl.when(has_left)
    def _():
        rim_copy(False).wait_send()

    @pl.when(jnp.logical_not(owns))
    def _():
        main.wait_send()

    @pl.when(has_target)
    def _():
        extra.wait_send()


def matrices():
    lane = np.arange(128)
    group = lane % 8
    spread = np.zeros((128, 128 * (KF + KC) + 640 + 256 * KC), np.float32)
    for k in range(KF + KC):
        spread[8 * k + group, 128 * k + lane] = 1.0
    base = 128 * (KF + KC)
    for r in range(5):
        spread[8 * (lane // 8) + r, base + 128 * r + lane] = 1.0
    base += 640
    for j in range(2):
        for k in range(KC):
            spread[64 * j + 4 + KC * group + k, base + 128 * (KC * j + k) + lane] = 2.0
    gather = np.zeros((128 * (KF + KC), 32), np.float32)
    for k in range(KF + KC):
        target = (KF * group + k - 4) // 2 if k < KF else KC * group + (k - KF) - 4
        ok = (target >= 0) & (target < 32)
        gather[128 * k + lane[ok], target[ok]] = 1.0
    return jnp.asarray(spread, BF16), jnp.asarray(gather, BF16)


def body(
    node_fine,
    node_coarse,
    weight_fine,
    weight_coarse,
    mode_x,
    mode_y,
    mode_z,
    source_fine,
    source_coarse,
):
    hbm = pl.BlockSpec(memory_space=pl.ANY)
    fine = (KF, 4, 8, 128)
    coarse = (4, KC, 2, 8, 128)
    dma = pltpu.SemaphoreType.DMA

    def vmem(*shape, dtype=F32):
        return pltpu.VMEM(shape, dtype)

    wide = 128 * (KF + KC)
    scratch = [
        vmem(16, 32, 512),
        vmem(16, 64, 64),
        vmem(1, KL, dtype=jnp.int32),
        vmem(4, KL, dtype=jnp.int32),
        vmem(1, 1, dtype=jnp.int32),
        vmem(1, 4, dtype=jnp.int32),
        vmem(KL, 128),
        vmem(KL, 512),
        vmem(KL, 32),
        vmem(KP, 512),
        vmem(XPAD + 128 + XPAD, 128),
        vmem(32, 128),
        vmem(128, wide + 640 + 256 * KC, dtype=BF16),
        vmem(wide, 32, dtype=BF16),
        vmem(8, 128),
        vmem(MEMBERS, 8, 128),
        vmem(12, 32, 128),
        vmem(12, 32, 128),
        vmem(128 * KC, 128),
        vmem(128, KF * 128, dtype=BF16),
        vmem(128, KC * 512, dtype=BF16),
        vmem(256, KF * 128, dtype=BF16),
        vmem(256, KC * 256, dtype=BF16),
        vmem(XF + 6, *fine),
        vmem(XF + 5, *fine),
        vmem(XF + 4, *fine),
        vmem(XF + 4, *fine),
        vmem(XF + 4, *fine),
        vmem(XF + 4, *fine),
        vmem(XF + 2, *fine),
        vmem(XC + 6, *coarse),
        vmem(XC + 5, *coarse),
        vmem(XC + 4, *coarse),
        vmem(XC + 4, *coarse),
        vmem(XC + 4, *coarse),
        vmem(XC + 4, *coarse),
        vmem(XC + 2, *coarse),
        vmem(5, 8, 128),
        vmem(64, wide),
        dma((11,)),
        dma(()),
        dma(()),
        dma((2,)),
        dma((2,)),
        dma((2,)),
        dma((2,)),
    ]
    return pl.pallas_call(
        kernel,
        out_shape=jax.ShapeDtypeStruct((4, 16, 32), F32),
        in_specs=[hbm] * 11,
        out_specs=pl.BlockSpec(memory_space=pltpu.VMEM),
        scratch_shapes=scratch,
        compiler_params=pltpu.CompilerParams(
            collective_id=0, has_side_effects=True, vmem_limit_bytes=60 * 2**20
        ),
    )(
        node_fine,
        node_coarse,
        weight_fine.reshape(1, 1),
        weight_coarse.reshape(1, 4),
        mode_x,
        mode_y,
        mode_z,
        source_fine,
        jnp.transpose(source_coarse, (1, 2, 0)),
        *matrices(),
    )


def solution(mesh):
    return jax.shard_map(
        body,
        mesh=mesh,
        in_specs=(
            P("member", None),
            P("member", None),
            P("member"),
            P("member"),
            P(),
            P(),
            P(),
            P("tile", None, None),
            P(None, None, "tile"),
        ),
        out_specs=P("member", None, "tile"),
        check_vma=False,
    )
```

```python
import math

import jax
import jax.numpy as jnp
import numpy as np
from jax import lax
from jax.experimental import pallas as pl
from jax.experimental.pallas import tpu as pltpu
from jax.sharding import PartitionSpec as P

NODES = 9
SWEEPS = 3
CENTRE = 1.125
HALF_WIDTH = 0.875
SPREAD_RATIO = CENTRE / HALF_WIDTH
LOG2E = 1.0 / math.log(2.0)

F32 = jnp.float32
BF16 = jnp.bfloat16
MESH = pl.DeviceIdType.MESH

TILES = 8
MEMBERS = 16
KL = 12
KP = 16
XF = 8
XC = 4
KF = 9
KC = 5
XPAD = 8
OUTSIDE = -1024.0


def sweep_factors(sweep_count):
    previous = 1.0 / SPREAD_RATIO
    factors = []
    for _ in range(sweep_count - 1):
        current = 1.0 / (2.0 * SPREAD_RATIO - previous)
        factors.append((current * previous, 2.0 * current / HALF_WIDTH))
        previous = current
    return factors


(KEEP1, PUSH1), (KEEP2, PUSH2) = sweep_factors(SWEEPS)
FIRST = 1.0 / CENTRE
SHARE = (1.0 - FIRST) / FIRST
SECOND = PUSH1 * FIRST
BETA = KEEP1 / PUSH1 + SHARE
LEFT = (1.0 - PUSH1) * FIRST
A1 = FIRST + PUSH2 * (LEFT * (SHARE - BETA) - KEEP1 * FIRST)
A2 = (1.0 + KEEP2) * SECOND + PUSH2 * LEFT
A3 = PUSH2 * SECOND
R1 = A1 / A3
R2 = A2 / A3


def iota(shape, dim):
    return lax.broadcasted_iota(jnp.int32, shape, dim)


def halves(value):
    high = value.astype(BF16)
    return high, (value - high.astype(F32)).astype(BF16)


def thirds(value):
    high = value.astype(BF16)
    rest = value - high.astype(F32)
    middle = rest.astype(BF16)
    return high, middle, (rest - middle.astype(F32)).astype(BF16)


def cut(value, low, high, axis):
    return lax.slice_in_dim(value, low, high, axis=axis)


def node_values(index):
    value = jnp.zeros(index.shape, F32)
    for node in range(NODES):
        value = jnp.where(index == node, math.cos(math.pi * node / (NODES - 1)) * LOG2E, value)
    return value


def z_faces(c, masks):
    n = c.shape[0]
    wrap = c[n - 1 : n] + jnp.where(masks[3], 0.0, pltpu.roll(c[0:1], 7, 1))
    closed = jnp.where(masks[3], 0.0, wrap)
    inner = c[0 : n - 1] + c[1:n]
    down = jnp.where(masks[2], c[0:1], pltpu.roll(closed, 1, 1))
    up = jnp.concatenate([inner, wrap], 0)
    return jnp.concatenate([inner, closed], 0), up + jnp.concatenate([down, inner], 0)


def z_pull(face, v):
    n = v.shape[0]
    inner, wrap = face[0 : n - 1], face[n - 1 : n]
    up = jnp.concatenate([inner * v[1:n], wrap * pltpu.roll(v[0:1], 7, 1)], 0)
    down = jnp.concatenate([pltpu.roll(wrap * v[n - 1 : n], 1, 1), inner * v[0 : n - 1]], 0)
    return up + down


class Level:
    def __init__(self, ks, c, fx, fy, fz, inv, g, e):
        self.ks, self.c, self.fx, self.fy, self.fz = ks, c, fx, fy, fz
        self.inv, self.g, self.e = inv, g, e

    def set_up(self, n, rest, masks, hide):
        ks = self.ks
        c = [self.c[(n + 1,) + rest + (k,)] for k in range(ks)]
        wrap = c[ks - 1] + jnp.where(masks[1], 0.0, pltpu.roll(c[0], 127, 2))
        closed = jnp.where(masks[1], 0.0, wrap)
        down = jnp.where(masks[0], c[0], pltpu.roll(closed, 1, 2))
        for k in range(ks):
            upper = c[k] + self.c[(n + 2,) + rest + (k,)]
            next_face = c[k] + c[k + 1] if k < ks - 1 else wrap
            z_face, z_sum = z_faces(c[k], masks)
            total = ((self.fx[(n,) + rest + (k,)] + upper) + (next_face + down)) + z_sum
            turned = pltpu.reciprocal(total, approx=True)
            for mask in hide(k):
                turned = jnp.where(mask, 0.0, turned)
            self.fx[(n + 1,) + rest + (k,)] = upper
            self.fy[(n,) + rest + (k,)] = next_face if k < ks - 1 else closed
            self.fz[(n,) + rest + (k,)] = z_face
            self.inv[(n,) + rest + (k,)] = turned
            down = next_face

    def pull(self, v, n, shift, rest):
        ks = self.ks
        f = n + shift
        last = v[(n,) + rest + (ks - 1,)]
        wrap = self.fy[(f,) + rest + (ks - 1,)]
        down = pltpu.roll(wrap * last, 1, 2)
        out = []
        for k in range(ks):
            at = rest + (k,)
            here = v[(n,) + at]
            if k < ks - 1:
                face = self.fy[(f,) + at]
                after = v[(n,) + rest + (k + 1,)]
                up = face * after
                next_down = face * here
            else:
                up = wrap * pltpu.roll(v[(n,) + rest + (0,)], 127, 2)
                next_down = None
            across = self.fx[(f,) + at] * v[(n - 1,) + at] + self.fx[(f + 1,) + at] * v[(n + 1,) + at]
            out.append((across + (up + down)) + z_pull(self.fz[(f,) + at], here))
            down = next_down
        return out

    def sweep(self, n, rest):
        moved = self.pull(self.g, n + 1, 0, rest)
        for k in range(self.ks):
            at = (n + 1,) + rest + (k,)
            self.e[(n,) + rest + (k,)] = BETA * self.g[at] + moved[k] * self.inv[at]

    def finish(self, n, rest):
        moved = self.pull(self.e, n + 1, 1, rest)
        out = []
        for k in range(self.ks):
            at = (n + 2,) + rest + (k,)
            out.append(
                (R1 * self.g[at] + R2 * self.e[(n + 1,) + rest + (k,)]) + moved[k] * self.inv[at]
            )
        return out


def kernel(
    node_f,
    node_c,
    w_f,
    w_c,
    mode_x,
    mode_y,
    mode_z,
    src_f,
    src_c,
    spread,
    gather,
    out,
    fraw,
    craw,
    nodes_f,
    nodes_c,
    weight_f,
    weight_c,
    mx,
    my_in,
    mz,
    mpad,
    xt,
    zt,
    spread_v,
    gather_v,
    mine,
    known,
    packed,
    fgot,
    fcs,
    rhs_f,
    rhs_c,
    double_f,
    double_c,
    c_f,
    fx_f,
    fy_f,
    fz_f,
    inv_f,
    g_f,
    e_f,
    c_c,
    fx_c,
    fy_c,
    fz_c,
    inv_c,
    g_c,
    e_c,
    wlane,
    qbuf,
    local_sem,
    node_send,
    node_recv,
    main_sem,
    extra_sem,
    rim_send,
    rim_recv,
):
    me_m = lax.axis_index("member")
    me_t = lax.axis_index("tile")
    parity = lax.rem(me_m, 2)
    half = me_m // 2

    def to(member, tile):
        return {"member": member, "tile": tile}

    def bring(index, source, target):
        copy = pltpu.make_async_copy(source, target, local_sem.at[index])
        copy.start()
        return copy

    own_nodes = [
        bring(0, node_f, nodes_f),
        bring(1, node_c, nodes_c),
        bring(2, w_f, weight_f),
        bring(3, w_c, weight_c),
    ]
    barrier = pltpu.get_barrier_semaphore()

    def tell(device):
        pl.semaphore_signal(barrier, inc=1, device_id=device, device_id_type=MESH)

    for step in range(1, MEMBERS):
        tell(to(lax.rem(me_m + step, MEMBERS), me_t))
    aim = 4 * (half // 4) + lax.rem(half + me_t, 4)

    def aiming(strip):
        return to(2 * (4 * (me_t // 4) + lax.rem(me_t - strip + 2 * TILES, 4)) + parity, strip)

    owns = (half == me_t) & (aim == me_t)
    extra_source = half - 1 + 2 * parity
    extra_target = me_t + 1 - 2 * parity
    has_source = (extra_source >= 0) & (extra_source < TILES)
    at_home = (extra_target == half) & (aim == me_t)
    has_target = (extra_target >= 0) & (extra_target < TILES) & jnp.logical_not(at_home)
    waits_extra = has_source & jnp.logical_not(at_home)
    has_left = me_t > 0
    has_right = me_t < TILES - 1

    @pl.when(jnp.logical_not(owns))
    def _():
        tell(aiming(half))

    @pl.when(waits_extra)
    def _():
        tell(aiming(extra_source))

    @pl.when(has_left)
    def _():
        tell(to(me_m, me_t - 1))

    @pl.when(has_right)
    def _():
        tell(to(me_m, me_t + 1))

    own_f = bring(4, src_f, fraw)
    own_c = bring(5, src_c, craw.at[:, pl.ds(8, 32)])
    modes = [
        bring(6, mode_x, mx),
        bring(7, mode_y, my_in),
        bring(8, mode_z, mz),
        bring(9, spread, spread_v),
        bring(10, gather, gather_v),
    ]

    lanes = iota((8, 128), 1)
    subs = iota((8, 128), 0)
    group = lanes & 7
    masks = (group == 0, group == 7, subs == 0, subs == 7)
    low_edge = (group == 0) & (me_t == 0)
    high_edge = (group == 7) & (me_t == TILES - 1)

    for copy in own_nodes:
        copy.wait()
    mine[...] = jnp.zeros((8, 128), F32)
    mine[0:1, 0:KL] = node_values(nodes_f[...])
    mine[1:5, 0:KL] = node_values(nodes_c[...])
    row = iota((8, 128), 0)
    weights = jnp.where(row == 0, jnp.broadcast_to(weight_f[...].astype(F32), (8, 128)), 0.0)
    for r in range(4):
        own_weight = jnp.broadcast_to(weight_c[:, r : r + 1].astype(F32), (8, 128))
        weights = jnp.where(row == r + 1, own_weight, weights)
    mine[...] = jnp.where(lanes == 15, weights, mine[...])

    def count(flag):
        return flag.astype(jnp.int32)

    pl.semaphore_wait(
        barrier,
        MEMBERS
        - count(owns)
        + count(has_target)
        + count(has_left)
        + count(has_right),
    )

    def node_copy(step):
        return pltpu.make_async_remote_copy(
            src_ref=mine,
            dst_ref=known.at[me_m],
            send_sem=node_send,
            recv_sem=node_recv,
            device_id=to(lax.rem(me_m + step, MEMBERS), me_t),
            device_id_type=MESH,
        )

    for step in range(1, MEMBERS):
        node_copy(step).start()
    known[me_m] = mine[...]

    def rim_copy(rightwards):
        if rightwards:
            return pltpu.make_async_remote_copy(
                src_ref=src_c.at[:, pl.ds(24, 8)],
                dst_ref=craw.at[:, pl.ds(0, 8)],
                send_sem=rim_send.at[0],
                recv_sem=rim_recv.at[0],
                device_id=to(me_m, lax.rem(me_t + 1, TILES)),
                device_id_type=MESH,
            )
        return pltpu.make_async_remote_copy(
            src_ref=src_c.at[:, pl.ds(0, 8)],
            dst_ref=craw.at[:, pl.ds(40, 8)],
            send_sem=rim_send.at[1],
            recv_sem=rim_recv.at[1],
            device_id=to(me_m, lax.rem(me_t + TILES - 1, TILES)),
            device_id_type=MESH,
        )

    @pl.when(has_right)
    def _():
        rim_copy(True).start()

    @pl.when(has_left)
    def _():
        rim_copy(False).start()

    craw[:, 48:64, :] = jnp.zeros((16, 16, 64), F32)

    @pl.when(jnp.logical_not(has_left))
    def _():
        craw[:, 0:8, :] = jnp.zeros((16, 8, 64), F32)

    @pl.when(jnp.logical_not(has_right))
    def _():
        craw[:, 40:48, :] = jnp.zeros((16, 8, 64), F32)

    own_f.wait()
    y = iota((512, 128), 0)
    col = iota((512, 128), 1)
    wanted = 64 * aim - 4 + KF * (col & 7) + (col >> 3)
    window = jnp.where((y == wanted) & (col < 8 * KF), 2.0, 0.0).astype(BF16)

    def pack(first, planes, at):
        high, low = halves(fraw[pl.ds(first, planes)].reshape(32 * planes, 512))
        got = jnp.dot(high, window, preferred_element_type=F32)
        got = got + jnp.dot(low, window, preferred_element_type=F32)
        packed[at : at + planes] = got.reshape(planes, 32, 128)

    pack(6 * parity, 10, 0)
    pack(14 - 14 * parity, 2, 10)

    main = pltpu.make_async_remote_copy(
        src_ref=packed.at[pl.ds(0, 10)],
        dst_ref=fgot.at[pl.ds(2 - 2 * parity, 10)],
        send_sem=main_sem.at[0],
        recv_sem=main_sem.at[1],
        device_id=to(2 * me_t + parity, aim),
        device_id_type=MESH,
    )
    extra = pltpu.make_async_remote_copy(
        src_ref=packed.at[pl.ds(10, 2)],
        dst_ref=fgot.at[pl.ds(10 * parity, 2)],
        send_sem=extra_sem.at[0],
        recv_sem=extra_sem.at[1],
        device_id=to(lax.rem(2 * extra_target + parity + MEMBERS, MEMBERS), aim),
        device_id_type=MESH,
    )

    @pl.when(jnp.logical_not(owns))
    def _():
        main.start()

    @pl.when(owns)
    def _():
        fgot[pl.ds(2 - 2 * parity, 10)] = packed[0:10]

    @pl.when(has_target)
    def _():
        extra.start()

    @pl.when(at_home)
    def _():
        fgot[pl.ds(10 * parity, 2)] = packed[10:12]

    @pl.when(jnp.logical_not(has_source))
    def _():
        fgot[pl.ds(10 * parity, 2)] = jnp.zeros((2, 32, 128), F32)

    for copy in modes:
        copy.wait()
    mpad[...] = jnp.zeros(mpad.shape, F32)
    mpad[0:KL, :] = my_in[...]
    fine_y = 64 * me_t - 4 + KF * (col & 7) + (col >> 3)
    coarse_y = 32 * me_t - 4 + KC * (col & 7) + ((col >> 3) - KF)
    picks = jnp.where(
        col < 8 * KF,
        jnp.where(y == fine_y, 1.0, 0.0),
        jnp.where(((y >> 1) == coarse_y) & (col < 8 * (KF + KC)), 0.5, 0.0),
    ).astype(BF16)
    parts = jnp.concatenate(thirds(mpad[...]), 0)
    my = jnp.dot(parts, picks, preferred_element_type=F32)
    my = (my[0:KP] + my[KP : 2 * KP]) + my[2 * KP : 3 * KP]
    own_col = iota((KP, 128), 1)
    fine_col = 64 * me_t - 4 + KF * (own_col & 7) + (own_col >> 3)
    coarse_col = 32 * me_t - 4 + KC * (own_col & 7) + ((own_col >> 3) - KF)
    reached = jnp.where(own_col < 8 * KF, fine_col, 2 * coarse_col)
    leaves = (reached < 0) | (reached >= 64 * TILES)
    my = jnp.where((iota((KP, 128), 0) == KL) & leaves, OUTSIDE, my)
    parts = jnp.concatenate(thirds(my), 0)
    wide = (KF + KC) * 128
    my = jnp.dot(parts, spread_v[:, 0:wide], preferred_element_type=F32)
    my = (my[0:KP] + my[KP : 2 * KP]) + my[2 * KP : 3 * KP]

    mpad[0:KL, 0:128] = mx[...]
    stacked = jnp.concatenate([mpad[:, 0:128]] * 8, 0)
    one = iota((XPAD, 128), 1)
    beyond = jnp.where((one == KL) | (one == KL + 1), 1.0, 0.0)
    xt[0:XPAD, :] = beyond
    xt[XPAD : XPAD + 128, :] = jnp.where(iota((128, 128), 1) == KL, 1.0, stacked.T)
    xt[XPAD + 128 : XPAD + 128 + XPAD, :] = beyond
    mpad[0:KL, 0:32] = mz[...]
    stacked = jnp.concatenate([mpad[:, 0:32]] * 8, 0)
    one = iota((32, 128), 1)
    zt[...] = jnp.where((one == KL) | (one == KL + 1), 1.0, stacked.T)
    zf = [zt[pl.ds(j, 8, stride=4), :] for j in range(4)]
    zc = [0.5 * (zf[2 * j] + zf[2 * j + 1]) for j in range(2)]
    zf = jnp.concatenate(zf, 0)
    zc = jnp.concatenate(zc, 0)

    def left(value):
        high = value.astype(BF16).astype(F32)
        return jnp.where(iota(value.shape, 1) < 32, high, value - high).astype(BF16)

    x0 = XF * me_m
    lhs_f = jnp.concatenate(
        [left(xt[pl.ds(x0 - 3 + XPAD + i, 1), :] * zf) for i in range(XF + 6)], 0
    )
    rows = []
    for i in range(XC + 6):
        at = x0 - 6 + XPAD + 2 * i
        mean = 0.5 * (xt[pl.ds(at, 1), :] + xt[pl.ds(at + 1, 1), :])
        rows.append(left(mean * zc))
    lhs_c = jnp.concatenate(rows, 0)
    rhs_f[64:128, :] = jnp.zeros((64, KF * 128), BF16)
    rhs_c[64:128, :] = jnp.zeros((64, KC * 512), BF16)

    wide_end = wide + 640
    for part in range(2):
        double_f[128 * part : 128 * part + 128, :] = spread_v[:, 0 : KF * 128]
        double_c[128 * part : 128 * part + 128, :] = spread_v[:, wide_end : wide_end + KC * 256]

    arrivals = pltpu.make_async_remote_copy(
        src_ref=known.at[pl.ds(0, MEMBERS - 1)],
        dst_ref=known.at[pl.ds(0, MEMBERS - 1)],
        send_sem=node_send,
        recv_sem=node_recv,
        device_id=to(lax.rem(me_m + 1, MEMBERS), me_t),
        device_id_type=MESH,
    )
    arrivals.wait_recv()
    turned = known[...].reshape(128, 128).T[0:KP]
    parts = jnp.concatenate(thirds(turned), 0)
    pick = spread_v[:, wide : wide + 640]
    values = jnp.dot(parts, pick, preferred_element_type=F32)
    values = (values[0:KP] + values[KP : 2 * KP]) + values[2 * KP : 3 * KP]
    for r in range(5):
        scale = 0.125 * A3 if r == 0 else A3
        wlane[r] = jnp.broadcast_to(values[15:16, 128 * r : 128 * r + 128] * scale, (8, 128))

    def sides(value, factor):
        row = iota(value.shape, 0)
        scaled = jnp.where(row == KL, value, value * factor)
        high, low = halves(jnp.where(row == KL + 1, OUTSIDE, scaled))
        return jnp.concatenate([high, low, high, low], 0)

    for k in range(KF):
        at = slice(128 * k, 128 * k + 128)
        rhs_f[0:64, at] = sides(my[:, at], values[:, 0:128])
    for r in range(4):
        for k in range(KC):
            rhs_c[0:64, 128 * (KC * r + k) : 128 * (KC * r + k) + 128] = sides(
                my[:, 128 * (KF + k) : 128 * (KF + k) + 128],
                values[:, 128 * (r + 1) : 128 * (r + 1) + 128],
            )

    logs = jnp.dot(lhs_f, rhs_f[...], preferred_element_type=F32)
    for i in range(XF + 6):
        for k in range(KF):
            c_f[i, k] = jnp.exp2(
                logs[32 * i : 32 * i + 32, 128 * k : 128 * k + 128]
            ).reshape(4, 8, 128)
    logs = jnp.dot(lhs_c, rhs_c[...], preferred_element_type=F32)
    for i in range(XC + 6):
        for r in range(4):
            for k in range(KC):
                at = 128 * (KC * r + k)
                c_c[i, r, k] = jnp.exp2(logs[16 * i : 16 * i + 16, at : at + 128]).reshape(2, 8, 128)

    fine = Level(KF, c_f, fx_f, fy_f, fz_f, inv_f, g_f, e_f)
    coarse = Level(KC, c_c, fx_c, fy_c, fz_c, inv_c, g_c, e_c)

    def hide_fine(k):
        return ([low_edge] if k < 4 else []) + ([high_edge] if k >= 5 else [])

    def hide_coarse(k):
        return ([low_edge] if k < 4 else []) + ([high_edge] if k >= 1 else [])

    def clear(inv, planes):
        @pl.when(me_m == 0)
        def _():
            inv[0:2] = jnp.zeros((2,) + inv.shape[1:], F32)

        @pl.when(me_m == MEMBERS - 1)
        def _():
            inv[planes - 2 : planes] = jnp.zeros((2,) + inv.shape[1:], F32)

    fx_f[0] = c_f[0] + c_f[1]
    fx_c[0] = c_c[0] + c_c[1]

    def set_fine(n, carry):
        fine.set_up(n, (), masks, hide_fine)
        return carry

    lax.fori_loop(0, XF + 4, set_fine, 0, unroll=4)
    clear(inv_f, XF + 4)

    def set_coarse(n, carry):
        for r in range(4):
            coarse.set_up(n, (r,), masks, hide_coarse)
        return carry

    lax.fori_loop(0, XC + 4, set_coarse, 0, unroll=4)
    clear(inv_c, XC + 4)

    @pl.when(jnp.logical_not(owns))
    def _():
        main.wait_recv()

    @pl.when(waits_extra)
    def _():
        extra.wait_recv()

    for chunk in range(3):
        rows = []
        for i in range(4):
            for j in range(4):
                rows.append(fgot[4 * chunk + i, pl.ds(j, 8, stride=4), :])
        high, low = halves(jnp.concatenate(rows, 0))
        got = jnp.dot(
            jnp.concatenate([high, low], 1), double_f[...], preferred_element_type=F32
        )
        for i in range(4):
            n = 4 * chunk + i
            for k in range(KF):
                g_f[n, k] = (
                    got[32 * i : 32 * i + 32, 128 * k : 128 * k + 128].reshape(4, 8, 128) * inv_f[n, k]
                )

    own_c.wait()

    @pl.when(has_left)
    def _():
        rim_copy(True).wait_recv()

    @pl.when(has_right)
    def _():
        rim_copy(False).wait_recv()

    chosen = (iota((16, 64), 1) == 4 * me_m - 2 + iota((16, 64), 0)) & (iota((16, 64), 0) < 8)
    chosen = jnp.where(chosen, 1.0, 0.0).astype(BF16)
    contract = (((1,), (1,)), ((), ()))
    planes = 0.0
    for part in halves(craw[...].reshape(1024, 64)):
        planes = planes + lax.dot_general(chosen, part, contract, preferred_element_type=F32)
    rows = jnp.concatenate([planes[0:8, 128 * p : 128 * p + 128] for p in range(8)], 0)
    high, low = halves(rows)
    got = jnp.dot(jnp.concatenate([high, low], 1), double_c[...], preferred_element_type=F32)
    for p in range(8):
        for j in range(2):
            for k in range(KC):
                at = 128 * (KC * j + k)
                fcs[pl.ds(16 * k + 8 * j + p, 8, stride=16 * KC), :] = got[
                    8 * p : 8 * p + 8, at : at + 128
                ]
    for n in range(XC + 4):
        for k in range(KC):
            at = 16 * (KC * n + k)
            source = fcs[at : at + 16, :].reshape(2, 8, 128)
            for r in range(4):
                g_c[n, r, k] = source * inv_c[n, r, k]

    def sweep_fine(n, carry):
        fine.sweep(n, ())
        return carry

    lax.fori_loop(0, XF + 2, sweep_fine, 0, unroll=1)

    def sweep_coarse(n, carry):
        for r in range(4):
            coarse.sweep(n, (r,))
        return carry

    lax.fori_loop(0, XC + 2, sweep_coarse, 0, unroll=2)

    def finish(xc, carry):
        base = pl.multiple_of(16 * xc, 16)
        n = 2 * xc
        low, high = fine.pull(e_f, n + 1, 1, ()), fine.pull(e_f, n + 2, 1, ())
        for k in range(KF):
            third = low[k] * inv_f[n + 2, k] + high[k] * inv_f[n + 3, k]
            first = g_f[n + 2, k] + g_f[n + 3, k]
            second = e_f[n + 1, k] + e_f[n + 2, k]
            for j in range(2):
                at = (2 * j, 2 * j + 1)
                total = (
                    R1 * (first[at[0]] + first[at[1]]) + R2 * (second[at[0]] + second[at[1]])
                ) + (third[at[0]] + third[at[1]])
                qbuf[pl.ds(base + 8 * j, 8), 128 * k : 128 * k + 128] = wlane[0] * total
        terms = [coarse.finish(xc, (r,)) for r in range(4)]
        for k in range(KC):
            at = 128 * (KF + k)
            both = (wlane[1] * terms[0][k] + wlane[2] * terms[1][k]) + (
                wlane[3] * terms[2][k] + wlane[4] * terms[3][k]
            )
            qbuf[pl.ds(base, 16), at : at + 128] = both.reshape(16, 128)
        return carry

    lax.fori_loop(0, XC, finish, 0)

    high, low = halves(qbuf[...])
    total = jnp.dot(high, gather_v[...], preferred_element_type=F32)
    total = total + jnp.dot(low, gather_v[...], preferred_element_type=F32)
    for xc in range(XC):
        for j in range(2):
            at = 16 * xc + 8 * j
            out[xc, pl.ds(j, 8, stride=2), :] = total[at : at + 8, 0:32]

    arrivals.wait_send()

    @pl.when(has_right)
    def _():
        rim_copy(True).wait_send()

    @pl.when(has_left)
    def _():
        rim_copy(False).wait_send()

    @pl.when(jnp.logical_not(owns))
    def _():
        main.wait_send()

    @pl.when(has_target)
    def _():
        extra.wait_send()


def matrices():
    lane = np.arange(128)
    group = lane % 8
    spread = np.zeros((128, 128 * (KF + KC) + 640 + 256 * KC), np.float32)
    for k in range(KF + KC):
        spread[8 * k + group, 128 * k + lane] = 1.0
    base = 128 * (KF + KC)
    for r in range(5):
        spread[8 * (lane // 8) + r, base + 128 * r + lane] = 1.0
    base += 640
    for j in range(2):
        for k in range(KC):
            spread[64 * j + 4 + KC * group + k, base + 128 * (KC * j + k) + lane] = 2.0
    gather = np.zeros((128 * (KF + KC), 32), np.float32)
    for k in range(KF + KC):
        target = (KF * group + k - 4) // 2 if k < KF else KC * group + (k - KF) - 4
        ok = (target >= 0) & (target < 32)
        gather[128 * k + lane[ok], target[ok]] = 1.0
    return jnp.asarray(spread, BF16), jnp.asarray(gather, BF16)


def body(
    node_fine,
    node_coarse,
    weight_fine,
    weight_coarse,
    mode_x,
    mode_y,
    mode_z,
    source_fine,
    source_coarse,
):
    hbm = pl.BlockSpec(memory_space=pl.ANY)
    fine = (KF, 4, 8, 128)
    coarse = (4, KC, 2, 8, 128)
    dma = pltpu.SemaphoreType.DMA

    def vmem(*shape, dtype=F32):
        return pltpu.VMEM(shape, dtype)

    wide = 128 * (KF + KC)
    scratch = [
        vmem(16, 32, 512),
        vmem(16, 64, 64),
        vmem(1, KL, dtype=jnp.int32),
        vmem(4, KL, dtype=jnp.int32),
        vmem(1, 1, dtype=jnp.int32),
        vmem(1, 4, dtype=jnp.int32),
        vmem(KL, 128),
        vmem(KL, 512),
        vmem(KL, 32),
        vmem(KP, 512),
        vmem(XPAD + 128 + XPAD, 128),
        vmem(32, 128),
        vmem(128, wide + 640 + 256 * KC, dtype=BF16),
        vmem(wide, 32, dtype=BF16),
        vmem(8, 128),
        vmem(MEMBERS, 8, 128),
        vmem(12, 32, 128),
        vmem(12, 32, 128),
        vmem(128 * KC, 128),
        vmem(128, KF * 128, dtype=BF16),
        vmem(128, KC * 512, dtype=BF16),
        vmem(256, KF * 128, dtype=BF16),
        vmem(256, KC * 256, dtype=BF16),
        vmem(XF + 6, *fine),
        vmem(XF + 5, *fine),
        vmem(XF + 4, *fine),
        vmem(XF + 4, *fine),
        vmem(XF + 4, *fine),
        vmem(XF + 4, *fine),
        vmem(XF + 2, *fine),
        vmem(XC + 6, *coarse),
        vmem(XC + 5, *coarse),
        vmem(XC + 4, *coarse),
        vmem(XC + 4, *coarse),
        vmem(XC + 4, *coarse),
        vmem(XC + 4, *coarse),
        vmem(XC + 2, *coarse),
        vmem(5, 8, 128),
        vmem(64, wide),
        dma((11,)),
        dma(()),
        dma(()),
        dma((2,)),
        dma((2,)),
        dma((2,)),
        dma((2,)),
    ]
    return pl.pallas_call(
        kernel,
        out_shape=jax.ShapeDtypeStruct((4, 16, 32), F32),
        in_specs=[hbm] * 11,
        out_specs=pl.BlockSpec(memory_space=pltpu.VMEM),
        scratch_shapes=scratch,
        compiler_params=pltpu.CompilerParams(
            collective_id=0, has_side_effects=True, vmem_limit_bytes=60 * 2**20
        ),
    )(
        node_fine,
        node_coarse,
        weight_fine.reshape(1, 1),
        weight_coarse.reshape(1, 4),
        mode_x,
        mode_y,
        mode_z,
        source_fine,
        jnp.transpose(source_coarse, (1, 2, 0)),
        *matrices(),
    )


def solution(mesh):
    return jax.shard_map(
        body,
        mesh=mesh,
        in_specs=(
            P("member", None),
            P("member", None),
            P("member"),
            P("member"),
            P(),
            P(),
            P(),
            P("tile", None, None),
            P(None, None, "tile"),
        ),
        out_specs=P("member", None, "tile"),
        check_vma=False,
    )
```
